128 devices in a mesh: frames: 8 (over y_lo, x), rows: 16 (over z, y_hi, core).
Axes of the slice: x: 4, y: 4 (y_hi: 2, y_lo: 2; y = y_hi * 2 + y_lo), z: 4, core: 2. Of those that a mesh axis runs over, the one named last changes fastest.
Arguments:
- latents: bfloat16 [15360, 128], P(('frames', 'rows')), may hold values from -6 to 6
- conv_in_weight: bfloat16 [432, 384], replicated, may hold values from -0.3125 to 0.3125
- gain: float32 [384], replicated, may hold values from 0.1 to 1.9
- conv_mid_weight: bfloat16 [10368, 384], replicated, may hold values from -0.0625 to 0.0625
- up_weight: bfloat16 [3456, 192], replicated, may hold values from -0.109375 to 0.109375
Outputs:
- upsampled: bfloat16 [8, 192, 61440], P('frames', 'rows')
The draws below stay inside these ranges and needn't reach their ends.
All inputs are finite; a program needn't handle non-finite values.
Results may differ from the reference program's by a relative error of at most 0.009.
Values may be sent and summed in bfloat16 or wider, within the bound.
A program may use at most 128 MiB of HBM per device.

```python
import jax
import jax.numpy as jnp
from jax import lax

C_LAT = 16
C = 384
C_UP = 192
W = 160
RD = 6
TOKENS = 30720
N_FRAMES = 8
N_ROWS = 16


def shard_levels(key, shape, pieces, least, high):
    level = 1.0
    for axis_at, shards_of in pieces:
        steps = jax.random.uniform(jax.random.fold_in(jax.random.fold_in(key, 6), axis_at), (shards_of,), jnp.float32, least / len(pieces), high / len(pieces))
        level = level * jnp.repeat(jnp.exp(steps), shape[axis_at] // shards_of).reshape((-1,) + (1,) * (len(shape) - 1 - axis_at))
    return level


def gaussian(key, shape, width, most, pieces=(), held_as=jnp.bfloat16):
    values = jax.random.normal(key, shape, jnp.float32) * width
    if len(pieces) > 0:
        values = shard_levels(key, shape, pieces, -0.22, 0.18) * values
    return jnp.clip(values, min=-most, max=most).astype(held_as)


def setup_inputs(seed: int = 0) -> dict:
    key_of = jax.random.split(jax.random.key(seed), 6)
    return {
        "latents": gaussian(key_of[0], (TOKENS // 2, 8 * C_LAT), 1.0, 6.0, ((0, 128),)),
        "conv_in_weight": gaussian(key_of[1], (27 * C_LAT, C), (27 * C_LAT) ** -0.5, 0.3125),
        "gain": jnp.clip(1.0 + 0.18 * jax.random.normal(key_of[2], (C,), jnp.float32), 0.1, 1.9),
        "conv_mid_weight": gaussian(key_of[3], (27 * C, C), (27 * C) ** -0.5, 0.0625),
        "up_weight": gaussian(key_of[4], (9 * C, C_UP), (9 * C) ** -0.5, 0.109375),
    }


def causal_conv(field, weight, in_channels):
    kernel = weight.astype(jnp.float32).reshape(3, 3, 3, in_channels, -1)
    result = lax.conv_general_dilated(field.astype(jnp.float32)[None], kernel, (1, 1, 1), [(2, 0), (1, 1), (1, 1)], dimension_numbers=('NDHWC', 'DHWIO', 'NDHWC'), precision=lax.Precision.HIGHEST)
    return result[0]

def silu_norm(first, gain):
    values = first.astype(jnp.float32)
    scale = lax.rsqrt(lax.optimization_barrier(jnp.mean(values * values, axis=-1, keepdims=True)) + 1e-06)
    return jax.nn.silu(values * scale * gain.astype(jnp.float32)).astype(jnp.bfloat16)

def reference(latents, conv_in_weight, gain, conv_mid_weight, up_weight):
    height = RD * N_ROWS
    video = latents.reshape(N_FRAMES, height // 2, W // 2, 2, 2, C_LAT).transpose(0, 1, 3, 2, 4, 5).reshape(N_FRAMES, height, W, C_LAT)
    first = causal_conv(video, conv_in_weight, C_LAT).astype(jnp.bfloat16)
    normed = silu_norm(first, gain)
    second = causal_conv(normed, conv_mid_weight, C)
    mixed = (first.astype(jnp.float32) + second).astype(jnp.bfloat16)
    kernel = up_weight.astype(jnp.float32).reshape(3, 3, C, C_UP)

    def one_frame(frame):
        big = jnp.repeat(jnp.repeat(frame, 2, axis=0), 2, axis=1).astype(jnp.float32)
        result = lax.conv_general_dilated(big[None], kernel, (1, 1), [(1, 1), (1, 1)], dimension_numbers=('NHWC', 'HWIO', 'NHWC'), precision=lax.Precision.HIGHEST)
        return result[0].reshape(2 * height, 2 * W * C_UP).astype(jnp.bfloat16)
    return lax.map(one_frame, mixed)
```

```python
import functools

import jax
import jax.numpy as jnp
from jax import lax
from jax.experimental import pallas as pl
from jax.experimental.pallas import tpu as pltpu
from jax.sharding import PartitionSpec as P

F32 = jnp.float32
BF16 = jnp.bfloat16
MESH = pl.DeviceIdType.MESH
C = 384
C_UP = 192
BACK = 4
HALF = 80
TOKEN_ROW = 40


def peers():
    return [(k, d) for k in range(BACK + 1) for d in (-1, 0, 1) if (k, d) != (0, 0)]


def exchange_kernel(frames, rows, x_ref, t_ref, own, above, below, spread, send_sem, recv_sem):
    f, r = lax.axis_index("frames"), lax.axis_index("rows")

    def target_ok(k, d):
        return (f + k < frames) & (r + d >= 0) & (r + d < rows)

    def source_ok(k, d):
        return (f - k >= 0) & (r - d >= 0) & (r - d < rows)

    barrier = pltpu.get_barrier_semaphore()
    for k, d in peers():

        @pl.when(source_ok(k, d))
        def _(k=k, d=d):
            pl.semaphore_signal(barrier, inc=1, device_id=(f - k, r - d), device_id_type=MESH)

    def as_int(flag):
        return jnp.where(flag, 1, 0)

    sides = 1 + as_int(r > 0) + as_int(r < rows - 1)
    later = 1 + jnp.minimum(frames - 1 - f, BACK)
    pl.semaphore_wait(barrier, sides * later - 1)

    def copy(n, k, d):
        if d == 0:
            src, dst = x_ref, own.at[k - 1]
        elif d == 1:
            src, dst = x_ref.at[TOKEN_ROW:], above.at[k]
        else:
            src, dst = x_ref.at[: 2 * TOKEN_ROW], below.at[k]
        return pltpu.make_async_remote_copy(
            src_ref=src,
            dst_ref=dst,
            send_sem=send_sem.at[n],
            recv_sem=recv_sem.at[n],
            device_id=(f + k, r + d),
            device_id_type=MESH,
        )

    for n, (k, d) in enumerate(peers()):

        @pl.when(target_ok(k, d))
        def _(n=n, k=k, d=d):
            copy(n, k, d).start()

    lane = lax.broadcasted_iota(jnp.int32, (128, 512), 0)
    spot = lax.broadcasted_iota(jnp.int32, (128, 512), 1)
    column = 2 * (lane // 64) + (lane // 16) % 2
    window = (spot // 16) % 4 - column
    part = spot // 128
    wanted = jnp.where(part == 0, 1, jnp.where(part == 1, -1, jnp.where(part == 2, -3, 3)))
    same = ((lane // 32) % 2 == (spot // 64) % 2) & (lane % 16 == spot % 16)
    select = jnp.where(same & (window == wanted), 1.0, 0.0).astype(BF16)

    def unfold(block, h, first_row):
        count = block.shape[0]
        got = jnp.dot(block, select, preferred_element_type=F32)
        at = lax.broadcasted_iota(jnp.int32, (count, 128), 0) % TOKEN_ROW
        left = jnp.where(at == 0, 0.0, pltpu.roll(got[:, 256:384], 1, 0))
        right = jnp.where(at == TOKEN_ROW - 1, 0.0, pltpu.roll(got[:, 384:], count - 1, 0))
        spread[pl.ds(0, count, stride=2), :] = got[:, :128] + left
        spread[pl.ds(1, count, stride=2), :] = got[:, 128:256] + right
        t_ref[h, first_row * HALF : first_row * HALF + 2 * count, :] = spread[
            : 2 * count, :
        ].astype(BF16)

    unfold(x_ref[...], BACK, 2)
    for n, (k, d) in enumerate(peers()):
        dst = own.at[k - 1] if d == 0 else above.at[k] if d == 1 else below.at[k]
        ok = source_ok(k, d)

        @pl.when(ok)
        def _(n=n, k=k, d=d):
            copy(n, k, d).wait_recv()

        @pl.when(jnp.logical_not(ok))
        def _(dst=dst):
            dst[...] = jnp.zeros_like(dst)

        unfold(dst[...], BACK - k, 2 if d == 0 else 0 if d == 1 else 5)
    for n, (k, d) in enumerate(peers()):

        @pl.when(target_ok(k, d))
        def _(n=n, k=k, d=d):
            copy(n, k, d).wait_send()


def exchange(latents, frames, rows):
    n = len(peers())
    return pl.pallas_call(
        functools.partial(exchange_kernel, frames, rows),
        out_shape=jax.ShapeDtypeStruct((BACK + 1, 7 * HALF, 128), BF16),
        in_specs=[pl.BlockSpec(memory_space=pltpu.VMEM)],
        out_specs=pl.BlockSpec(memory_space=pltpu.VMEM),
        scratch_shapes=[
            pltpu.VMEM((BACK, 3 * TOKEN_ROW, 128), BF16),
            pltpu.VMEM((BACK + 1, 2 * TOKEN_ROW, 128), BF16),
            pltpu.VMEM((BACK + 1, 2 * TOKEN_ROW, 128), BF16),
            pltpu.VMEM((6 * TOKEN_ROW, 128), F32),
            pltpu.SemaphoreType.DMA((n,)),
            pltpu.SemaphoreType.DMA((n,)),
        ],
        compiler_params=pltpu.CompilerParams(
            collective_id=0, has_side_effects=True, vmem_limit_bytes=16 * 2**20
        ),
        name="exchange",
    )(latents)


def decode_kernel(
    rows,
    t_ref, gain_ref, w_in_ref, w_mid_hbm, w_up_hbm, o_ref,
    w_mid, w_up, w_first, w_phase, z, first, n0, n1, n1m, n0p, acc0, acc1, turned, sems,
):
    r = lax.axis_index("rows")
    top = jnp.where(r == 0, 0.0, 1.0)
    bottom = jnp.where(r == rows - 1, 0.0, 1.0)

    up_copy = pltpu.make_async_copy(w_up_hbm, w_up, sems.at[3])
    up_copy.start()
    mid_copies = [
        pltpu.make_async_copy(
            w_mid_hbm.at[a * 9 * C : (a + 1) * 9 * C], w_mid.at[a * 9 * C : (a + 1) * 9 * C], sems.at[a]
        )
        for a in range(3)
    ]
    for copy in mid_copies:
        copy.start()

    for a in range(3):
        for at, rho in enumerate((3, 0, 1, 2)):
            for kappa in range(4):
                start = a * 256 + at * 64 + kappa * 16
                for p in range(2):
                    for q in range(2):
                        b, e = rho - p, kappa - q
                        spot = (slice(start, start + 16), slice((2 * p + q) * C, (2 * p + q + 1) * C))
                        if 0 <= b <= 2 and 0 <= e <= 2:
                            tap = ((a * 3 + b) * 3 + e) * 16
                            w_first[spot] = w_in_ref[tap : tap + 16, :]
                        else:
                            w_first[spot] = jnp.zeros((16, C), BF16)

    lower = lax.broadcasted_iota(jnp.int32, (5 * HALF, 128), 1) < 64
    for h in range(BACK + 1):
        z[h, :, :128] = jnp.where(lower, t_ref[h, 2 * HALF :, :], t_ref[h, : 5 * HALF, :])
        z[h, :, 128:] = t_ref[h, HALF : 6 * HALF, :]

    gain = gain_ref[...]
    at = lax.broadcasted_iota(jnp.int32, (HALF, C), 0)

    def shifted_right(values):
        return jnp.where(at == 0, 0.0, pltpu.roll(values, 1, 0)).astype(BF16)

    def shifted_left(values):
        return jnp.where(at == HALF - 1, 0.0, pltpu.roll(values, HALF - 1, 0)).astype(BF16)

    def first_step(g, carry):
        block = jnp.concatenate([z[g], z[g + 1], z[g + 2]], axis=1)
        for p in range(2):
            result = jnp.dot(
                block, w_first[:, 2 * p * C : 2 * (p + 1) * C], preferred_element_type=F32
            )
            for w in range(5):
                row = 2 * w + p
                spot = slice(row * HALF, (row + 1) * HALF)
                for q in range(2):
                    rounded = result[w * HALF : (w + 1) * HALF, q * C : (q + 1) * C].astype(BF16)
                    first[q, spot, :] = rounded
                    value = rounded.astype(F32)
                    scale = lax.rsqrt(jnp.mean(value * value, axis=-1, keepdims=True) + 1e-6)
                    if row < 2:
                        scale = scale * top
                    if row >= 8:
                        scale = scale * bottom
                    value = value * scale * gain
                    value = value / (1.0 + jnp.exp(-value))
                    if q == 0:
                        n0[g, spot, :] = value.astype(BF16)
                        n0p[g, spot, :] = shifted_left(value)
                    else:
                        n1[g, spot, :] = value.astype(BF16)
                        n1m[g, spot, :] = shifted_right(value)
        return carry

    lax.fori_loop(0, 3, first_step, 0)

    up_copy.wait()
    met = (((0,), (1, 2)), ((0, 1), (2,)))
    for p in range(2):
        for q in range(2):
            for i in range(2):
                for j in range(2):
                    total = None
                    for b in met[p][i]:
                        for e in met[q][j]:
                            tap = (b * 3 + e) * C
                            term = w_up[tap : tap + C, :].astype(F32)
                            total = term if total is None else total + term
                    w_phase[2 * p + q, (2 * i + j) * C : (2 * i + j + 1) * C, :] = total.astype(BF16)

    for copy in mid_copies:
        copy.wait()

    M = 8 * HALF
    acc0[...] = jnp.zeros_like(acc0)
    acc1[...] = jnp.zeros_like(acc1)

    def mid_step(a, carry):
        base = a * 9 * C

        def tap(b, e):
            return w_mid[pl.ds(pl.multiple_of(base + (b * 3 + e) * C, C), C), :]

        def taken(*sources):
            return jnp.concatenate(
                [source[a, b * HALF : b * HALF + M, :] for b in range(3) for source in sources], axis=1
            )

        weight = jnp.concatenate(
            [
                jnp.concatenate([tap(b, 1 + k), tap(b, k)], axis=1)
                for b in range(3)
                for k in range(2)
            ],
            axis=0,
        )
        both = jnp.dot(taken(n0, n1), weight, preferred_element_type=F32)
        weight = jnp.concatenate([tap(b, 0) for b in range(3)], axis=0)
        acc0[...] += both[:, :C] + jnp.dot(taken(n1m), weight, preferred_element_type=F32)
        weight = jnp.concatenate([tap(b, 2) for b in range(3)], axis=0)
        acc1[...] += both[:, C:] + jnp.dot(taken(n0p), weight, preferred_element_type=F32)
        return carry

    lax.fori_loop(0, 3, mid_step, 0)

    for row in range(8):
        spot = slice(row * HALF, (row + 1) * HALF)
        source = slice((row + 1) * HALF, (row + 2) * HALF)
        for q, acc in enumerate((acc0, acc1)):
            value = acc[spot, :] + first[q, source, :].astype(F32)
            if row == 0:
                value = value * top
            if row == 7:
                value = value * bottom
            if q == 0:
                n0[0, spot, :] = value.astype(BF16)
                n0p[0, spot, :] = shifted_left(value)
            else:
                n1[0, spot, :] = value.astype(BF16)
                n1m[0, spot, :] = shifted_right(value)

    L = 6 * HALF
    columns = ((n1m, n0, n1), (n0, n1, n0p))
    for q in range(2):
        for p in range(2):
            halves = []
            for v in range(2):
                taken = jnp.concatenate(
                    [
                        source[0, (p + i) * HALF : (p + i) * HALF + L, :]
                        for i in range(2)
                        for source in columns[q][v : v + 2]
                    ],
                    axis=1,
                )
                halves.append(jnp.dot(taken, w_phase[2 * p + v], preferred_element_type=F32))
            whole = jnp.concatenate(halves, axis=1)
            for i in range(6):
                for t in range(3):
                    turned[pl.ds((q * 3 + t) * 16 + 2 * i + p, HALF, stride=96), :] = whole[
                        i * HALF : (i + 1) * HALF, t * 128 : (t + 1) * 128
                    ]

    def write(n, carry):
        for t in range(24):
            at_tile = n * 24 + t
            tile = turned[pl.ds(pl.multiple_of(at_tile * 16, 16), 16), :].astype(BF16)
            o_ref[0, :, pl.ds(pl.multiple_of(at_tile * 128, 128), 128)] = tile[:12, :]
        return carry

    lax.fori_loop(0, 20, write, 0)


def decode(tiles, gain, w_in, w_mid, w_up, rows):
    in_vmem = pl.BlockSpec(memory_space=pltpu.VMEM)
    in_hbm = pl.BlockSpec(memory_space=pl.ANY)
    return pl.pallas_call(
        functools.partial(decode_kernel, rows),
        out_shape=jax.ShapeDtypeStruct((1, 12, 2 * 160 * C_UP), BF16),
        in_specs=[in_vmem, in_vmem, in_vmem, in_hbm, in_hbm],
        out_specs=in_vmem,
        scratch_shapes=[
            pltpu.VMEM((27 * C, C), BF16),
            pltpu.VMEM((9 * C, C_UP), BF16),
            pltpu.VMEM((768, 4 * C), BF16),
            pltpu.VMEM((4, 4 * C, C_UP), BF16),
            pltpu.VMEM((BACK + 1, 5 * HALF, 256), BF16),
            pltpu.VMEM((2, 10 * HALF, C), BF16),
            *[pltpu.VMEM((3, 10 * HALF, C), BF16)] * 4,
            *[pltpu.VMEM((8 * HALF, C), F32)] * 2,
            pltpu.VMEM((160 * 3 * 16, 128), F32),
            pltpu.SemaphoreType.DMA((4,)),
        ],
        compiler_params=pltpu.CompilerParams(vmem_limit_bytes=60 * 2**20),
        name="decode",
    )(tiles, gain, w_in, w_mid, w_up)


def on_device(frames, rows, latents, conv_in_weight, gain, conv_mid_weight, up_weight):
    tiles = exchange(latents, frames, rows)
    return decode(tiles, gain.reshape(1, C), conv_in_weight, conv_mid_weight, up_weight, rows)


def solution(mesh):
    in_specs = (P(("frames", "rows"), None), P(), P(), P(), P())
    out_specs = P("frames", "rows", None)
    return jax.shard_map(
        functools.partial(on_device, mesh.shape["frames"], mesh.shape["rows"]),
        mesh=mesh,
        in_specs=in_specs,
        out_specs=out_specs,
        check_vma=False,
    )
```

```python
import functools

import jax
import jax.numpy as jnp
from jax import lax
from jax.experimental import pallas as pl
from jax.experimental.pallas import tpu as pltpu
from jax.sharding import PartitionSpec as P

F32 = jnp.float32
BF16 = jnp.bfloat16
MESH = pl.DeviceIdType.MESH
C = 384
C_UP = 192
BACK = 4
HALF = 80
TOKEN_ROW = 40


def peers():
    return [(k, d) for k in range(BACK + 1) for d in (-1, 0, 1) if (k, d) != (0, 0)]


def dot_t(left, right):
    return lax.dot_general(left, right, (((1,), (1,)), ((), ())), preferred_element_type=F32)


def decode_kernel(
    frames, rows,
    x_ref, w_in_hbm, gain_hbm, w_mid_hbm, w_up_hbm,
    o_ref,
    mine, w_in, gain, w_mid, w_up, w_first, w_phase,
    own, above, below, spread, tiles, z, first, n0, n1, n1m, n0p, acc0, acc1, turned,
    send_sem, recv_sem, load_sem,
):
    f, r = lax.axis_index("frames"), lax.axis_index("rows")

    def target_ok(k, d):
        return (f + k < frames) & (r + d >= 0) & (r + d < rows)

    def source_ok(k, d):
        return (f - k >= 0) & (r - d >= 0) & (r - d < rows)

    loads = [
        pltpu.make_async_copy(source, target, load_sem.at[n])
        for n, (source, target) in enumerate(
            (
                (x_ref, mine),
                (w_in_hbm, w_in),
                (w_up_hbm, w_up),
                (gain_hbm, gain.at[0]),
                (w_mid_hbm, w_mid),
            )
        )
    ]
    for load in loads:
        load.start()
    barrier = pltpu.get_barrier_semaphore()
    for k, d in peers():

        @pl.when(source_ok(k, d))
        def _(k=k, d=d):
            pl.semaphore_signal(barrier, inc=1, device_id=(f - k, r - d), device_id_type=MESH)

    lane = lax.broadcasted_iota(jnp.int32, (128, 512), 0)
    spot = lax.broadcasted_iota(jnp.int32, (128, 512), 1)
    column = 2 * (lane // 64) + (lane // 16) % 2
    window = (spot // 16) % 4 - column
    part = spot // 128
    wanted = jnp.where(part == 0, 1, jnp.where(part == 1, -1, jnp.where(part == 2, -3, 3)))
    same = ((lane // 32) % 2 == (spot // 64) % 2) & (lane % 16 == spot % 16)
    select = jnp.where(same & (window == wanted), 1.0, 0.0).astype(BF16)

    for k, d in peers():
        dst = own.at[k - 1] if d == 0 else above.at[k] if d == 1 else below.at[k]

        @pl.when(jnp.logical_not(source_ok(k, d)))
        def _(dst=dst):
            dst[...] = jnp.zeros_like(dst)

    def as_int(flag):
        return jnp.where(flag, 1, 0)

    sides = 1 + as_int(r > 0) + as_int(r < rows - 1)
    later = 1 + jnp.minimum(frames - 1 - f, BACK)
    pl.semaphore_wait(barrier, sides * later - 1)

    def copy(n, k, d):
        if d == 0:
            src, dst = x_ref, own.at[k - 1]
        elif d == 1:
            src, dst = x_ref.at[TOKEN_ROW:], above.at[k]
        else:
            src, dst = x_ref.at[: 2 * TOKEN_ROW], below.at[k]
        return pltpu.make_async_remote_copy(
            src_ref=src,
            dst_ref=dst,
            send_sem=send_sem.at[n],
            recv_sem=recv_sem.at[n],
            device_id=(f + k, r + d),
            device_id_type=MESH,
        )

    for n, (k, d) in enumerate(peers()):

        @pl.when(target_ok(k, d))
        def _(n=n, k=k, d=d):
            copy(n, k, d).start()

    def unfold(block, h, first_row):
        count = block.shape[0]
        got = jnp.dot(block, select, preferred_element_type=F32)
        at = lax.broadcasted_iota(jnp.int32, (count, 128), 0) % TOKEN_ROW
        left = jnp.where(at == 0, 0.0, pltpu.roll(got[:, 256:384], 1, 0))
        right = jnp.where(at == TOKEN_ROW - 1, 0.0, pltpu.roll(got[:, 384:], count - 1, 0))
        spread[pl.ds(0, count, stride=2), :] = got[:, :128] + left
        spread[pl.ds(1, count, stride=2), :] = got[:, 128:256] + right
        tiles[h, first_row * HALF : first_row * HALF + 2 * count, :] = spread[
            : 2 * count, :
        ].astype(BF16)

    loads[1].wait()
    for a in range(3):
        for at, rho in enumerate((3, 0, 1, 2)):
            for kappa in range(4):
                start = a * 256 + at * 64 + kappa * 16
                for p in range(2):
                    for q in range(2):
                        b, e = rho - p, kappa - q
                        spot = (slice(start, start + 16), slice((2 * p + q) * C, (2 * p + q + 1) * C))
                        if 0 <= b <= 2 and 0 <= e <= 2:
                            tap = ((a * 3 + b) * 3 + e) * 16
                            w_first[spot] = w_in[tap : tap + 16, :]
                        else:
                            w_first[spot] = jnp.zeros((16, C), BF16)

    loads[2].wait()
    met = (((0,), (1, 2)), ((0, 1), (2,)))
    for p in range(2):
        for q in range(2):
            for i in range(2):
                for j in range(2):
                    total = None
                    for b in met[p][i]:
                        for e in met[q][j]:
                            tap = (b * 3 + e) * C
                            term = w_up[:, tap : tap + C].astype(F32)
                            total = term if total is None else total + term
                    w_phase[2 * p + q, :, (2 * i + j) * C : (2 * i + j + 1) * C] = total.astype(BF16)

    top = jnp.where(r == 0, 0.0, 1.0)
    bottom = jnp.where(r == rows - 1, 0.0, 1.0)

    lower = lax.broadcasted_iota(jnp.int32, (5 * HALF, 128), 1) < 64
    def arrive(frames_back):
        for n, (k, d) in enumerate(peers()):
            if k not in frames_back:
                continue

            @pl.when(source_ok(k, d))
            def _(n=n, k=k, d=d):
                copy(n, k, d).wait_recv()

            dst = own.at[k - 1] if d == 0 else above.at[k] if d == 1 else below.at[k]
            unfold(dst[...], BACK - k, 2 if d == 0 else 0 if d == 1 else 5)
        for k in frames_back:
            h = BACK - k
            z[h, :, :128] = jnp.where(lower, tiles[h, 2 * HALF :, :], tiles[h, : 5 * HALF, :])
            z[h, :, 128:] = tiles[h, HALF : 6 * HALF, :]

    loads[0].wait()
    unfold(mine[...], BACK, 2)

    loads[3].wait()
    half_gain = 0.5 * gain[...]
    at = lax.broadcasted_iota(jnp.int32, (HALF, C), 0)

    def shifted_right(values):
        return jnp.where(at == 0, 0.0, pltpu.roll(values, 1, 0)).astype(BF16)

    def shifted_left(values):
        return jnp.where(at == HALF - 1, 0.0, pltpu.roll(values, HALF - 1, 0)).astype(BF16)

    def first_step(g):
        block = jnp.concatenate([z[g], z[g + 1], z[g + 2]], axis=1)
        for p in range(2):
            result = jnp.dot(
                block, w_first[:, 2 * p * C : 2 * (p + 1) * C], preferred_element_type=F32
            )
            for w in range(5):
                row = 2 * w + p
                spot = slice(row * HALF, (row + 1) * HALF)
                for q in range(2):
                    rounded = result[w * HALF : (w + 1) * HALF, q * C : (q + 1) * C].astype(BF16)
                    if g == 2:
                        first[q, spot, :] = rounded
                    value = rounded.astype(F32)
                    scale = lax.rsqrt(jnp.mean(value * value, axis=-1, keepdims=True) + 1e-6)
                    if row < 2:
                        scale = scale * top
                    if row >= 8:
                        scale = scale * bottom
                    value = value * scale * half_gain
                    value = value + value * jnp.tanh(value)
                    if q == 0:
                        n0[g, spot, :] = value.astype(BF16)
                        n0p[g, spot, :] = shifted_left(value)
                    else:
                        n1[g, spot, :] = value.astype(BF16)
                        n1m[g, spot, :] = shifted_right(value)

    arrive((0, 1, 2))
    first_step(2)
    arrive((3,))
    first_step(1)
    arrive((4,))
    first_step(0)

    for load in loads[4:]:
        load.wait()

    M = 8 * HALF
    acc0[...] = jnp.zeros_like(acc0)
    acc1[...] = jnp.zeros_like(acc1)

    def mid_step(a, carry):
        base = a * 9 * C

        def tap(b, e):
            return w_mid[pl.ds(pl.multiple_of(base + (b * 3 + e) * C, C), C), :]

        def taken(*sources):
            return jnp.concatenate(
                [source[a, b * HALF : b * HALF + M, :] for b in range(3) for source in sources], axis=1
            )

        weight = jnp.concatenate(
            [
                jnp.concatenate([tap(b, 1 + k), tap(b, k)], axis=1)
                for b in range(3)
                for k in range(2)
            ],
            axis=0,
        )
        both = jnp.dot(taken(n0, n1), weight, preferred_element_type=F32)
        weight = jnp.concatenate([tap(b, 0) for b in range(3)], axis=0)
        acc0[...] += both[:, :C] + jnp.dot(taken(n1m), weight, preferred_element_type=F32)
        weight = jnp.concatenate([tap(b, 2) for b in range(3)], axis=0)
        acc1[...] += both[:, C:] + jnp.dot(taken(n0p), weight, preferred_element_type=F32)
        return carry

    lax.fori_loop(0, 3, mid_step, 0)

    for row in range(8):
        spot = slice(row * HALF, (row + 1) * HALF)
        source = slice((row + 1) * HALF, (row + 2) * HALF)
        for q, acc in enumerate((acc0, acc1)):
            value = acc[spot, :] + first[q, source, :].astype(F32)
            if row == 0:
                value = value * top
            if row == 7:
                value = value * bottom
            if q == 0:
                n0[0, spot, :] = value.astype(BF16)
                n0p[0, spot, :] = shifted_left(value)
            else:
                n1[0, spot, :] = value.astype(BF16)
                n1m[0, spot, :] = shifted_right(value)

    L = 6 * HALF
    columns = ((n1m, n0, n1), (n0, n1, n0p))
    for q in range(2):
        for p in range(2):
            halves = []
            for v in range(2):
                taken = jnp.concatenate(
                    [
                        source[0, (p + i) * HALF : (p + i) * HALF + L, :]
                        for i in range(2)
                        for source in columns[q][v : v + 2]
                    ],
                    axis=1,
                )
                halves.append(dot_t(taken, w_phase[2 * p + v]))
            whole = jnp.concatenate(halves, axis=1)
            for i in range(6):
                for t in range(3):
                    turned[pl.ds((q * 3 + t) * 16 + 2 * i + p, HALF, stride=96), :] = whole[
                        i * HALF : (i + 1) * HALF, t * 128 : (t + 1) * 128
                    ]

    def write(n, carry):
        tiles = turned[pl.ds(pl.multiple_of(n * 24 * 16, 16), 24 * 16), :].astype(BF16)
        whole = jnp.concatenate([tiles[t * 16 : t * 16 + 12, :] for t in range(24)], axis=1)
        o_ref[0, :, pl.ds(pl.multiple_of(n * 24 * 128, 128), 24 * 128)] = whole
        return carry

    lax.fori_loop(0, 20, write, 0)

    for n, (k, d) in enumerate(peers()):

        @pl.when(target_ok(k, d))
        def _(n=n, k=k, d=d):
            copy(n, k, d).wait_send()


def on_device(frames, rows, latents, conv_in_weight, gain, conv_mid_weight, up_weight):
    n = len(peers())
    return pl.pallas_call(
        functools.partial(decode_kernel, frames, rows),
        out_shape=jax.ShapeDtypeStruct((1, 12, 2 * 160 * C_UP), BF16),
        in_specs=[pl.BlockSpec(memory_space=pl.ANY)] * 5,
        out_specs=pl.BlockSpec(memory_space=pltpu.VMEM),
        scratch_shapes=[
            pltpu.VMEM((3 * TOKEN_ROW, 128), BF16),
            pltpu.VMEM((432, C), BF16),
            pltpu.VMEM((1, C), F32),
            pltpu.VMEM((27 * C, C), BF16),
            pltpu.VMEM((C_UP, 9 * C), BF16),
            pltpu.VMEM((768, 4 * C), BF16),
            pltpu.VMEM((4, C_UP, 4 * C), BF16),
            pltpu.VMEM((BACK, 3 * TOKEN_ROW, 128), BF16),
            pltpu.VMEM((BACK + 1, 2 * TOKEN_ROW, 128), BF16),
            pltpu.VMEM((BACK + 1, 2 * TOKEN_ROW, 128), BF16),
            pltpu.VMEM((6 * TOKEN_ROW, 128), F32),
            pltpu.VMEM((BACK + 1, 7 * HALF, 128), BF16),
            pltpu.VMEM((BACK + 1, 5 * HALF, 256), BF16),
            pltpu.VMEM((2, 10 * HALF, C), BF16),
            *[pltpu.VMEM((3, 10 * HALF, C), BF16)] * 4,
            *[pltpu.VMEM((8 * HALF, C), F32)] * 2,
            pltpu.VMEM((160 * 3 * 16, 128), F32),
            pltpu.SemaphoreType.DMA((n,)),
            pltpu.SemaphoreType.DMA((n,)),
            pltpu.SemaphoreType.DMA((5,)),
        ],
        compiler_params=pltpu.CompilerParams(
            collective_id=0, has_side_effects=True, vmem_limit_bytes=60 * 2**20
        ),
        name="decode",
    )(latents, conv_in_weight, gain, conv_mid_weight, up_weight.T)


def solution(mesh):
    in_specs = (P(("frames", "rows"), None), P(), P(), P(), P())
    out_specs = P("frames", "rows", None)
    return jax.shard_map(
        functools.partial(on_device, mesh.shape["frames"], mesh.shape["rows"]),
        mesh=mesh,
        in_specs=in_specs,
        out_specs=out_specs,
        check_vma=False,
    )
```

```python
import functools

import jax
import jax.numpy as jnp
from jax import lax
from jax.experimental import pallas as pl
from jax.experimental.pallas import tpu as pltpu
from jax.sharding import PartitionSpec as P

F32 = jnp.float32
BF16 = jnp.bfloat16
MESH = pl.DeviceIdType.MESH
C = 384
C_UP = 192
BACK = 4
HALF = 80
MIX_LIMIT, UP_LIMIT = 58, 58
TOKEN_ROW = 40


def peers():
    return [(k, d) for k in range(BACK + 1) for d in (-1, 0, 1) if (k, d) != (0, 0)]


def dot_t(left, right):
    return lax.dot_general(left, right, (((1,), (1,)), ((), ())), preferred_element_type=F32)


def mix_kernel(
    frames, rows,
    x_ref, w_in_hbm, gain_hbm, w_mid_hbm, w_up_hbm,
    m0_hbm, m1_hbm, w_phase_hbm,
    mine, w_in, gain, w_mid, w_up, w_first, w_phase, w_pair, m0, m1,
    own, above, below, spread, tiles, z, first, n0, n1, result_a, result_b, sums,
    send_sem, recv_sem, load_sem, store_sem,
):
    f, r = lax.axis_index("frames"), lax.axis_index("rows")

    def target_ok(k, d):
        return (f + k < frames) & (r + d >= 0) & (r + d < rows)

    def source_ok(k, d):
        return (f - k >= 0) & (r - d >= 0) & (r - d < rows)

    loads = [
        pltpu.make_async_copy(source, target, load_sem.at[n])
        for n, (source, target) in enumerate(
            (
                (x_ref, mine),
                (w_in_hbm, w_in),
                (w_up_hbm, w_up),
                (gain_hbm, gain.at[0]),
                (w_mid_hbm, w_mid),
            )
        )
    ]
    for load in loads:
        load.start()
    barrier = pltpu.get_barrier_semaphore()
    for k, d in peers():

        @pl.when(source_ok(k, d))
        def _(k=k, d=d):
            pl.semaphore_signal(barrier, inc=1, device_id=(f - k, r - d), device_id_type=MESH)

    lane = lax.broadcasted_iota(jnp.int32, (128, 512), 0)
    spot = lax.broadcasted_iota(jnp.int32, (128, 512), 1)
    column = 2 * (lane // 64) + (lane // 16) % 2
    window = (spot // 16) % 4 - column
    part = spot // 128
    wanted = jnp.where(part == 0, 1, jnp.where(part == 1, -1, jnp.where(part == 2, -3, 3)))
    same = ((lane // 32) % 2 == (spot // 64) % 2) & (lane % 16 == spot % 16)
    select = jnp.where(same & (window == wanted), 1.0, 0.0).astype(BF16)

    for k, d in peers():
        dst = own.at[k - 1] if d == 0 else above.at[k] if d == 1 else below.at[k]

        @pl.when(jnp.logical_not(source_ok(k, d)))
        def _(dst=dst):
            dst[...] = jnp.zeros_like(dst)

    def as_int(flag):
        return jnp.where(flag, 1, 0)

    sides = 1 + as_int(r > 0) + as_int(r < rows - 1)
    later = 1 + jnp.minimum(frames - 1 - f, BACK)
    pl.semaphore_wait(barrier, sides * later - 1)

    def copy(n, k, d):
        if d == 0:
            src, dst = x_ref, own.at[k - 1]
        elif d == 1:
            src, dst = x_ref.at[TOKEN_ROW:], above.at[k]
        else:
            src, dst = x_ref.at[: 2 * TOKEN_ROW], below.at[k]
        return pltpu.make_async_remote_copy(
            src_ref=src,
            dst_ref=dst,
            send_sem=send_sem.at[n],
            recv_sem=recv_sem.at[n],
            device_id=(f + k, r + d),
            device_id_type=MESH,
        )

    for n, (k, d) in enumerate(peers()):

        @pl.when(target_ok(k, d))
        def _(n=n, k=k, d=d):
            copy(n, k, d).start()

    def unfold(block, h, first_row):
        count = block.shape[0]
        got = jnp.dot(block, select, preferred_element_type=F32)
        at = lax.broadcasted_iota(jnp.int32, (count, 128), 0) % TOKEN_ROW
        left = jnp.where(at == 0, 0.0, pltpu.roll(got[:, 256:384], 1, 0))
        right = jnp.where(at == TOKEN_ROW - 1, 0.0, pltpu.roll(got[:, 384:], count - 1, 0))
        spread[pl.ds(0, count, stride=2), :] = got[:, :128] + left
        spread[pl.ds(1, count, stride=2), :] = got[:, 128:256] + right
        for i in range(count // TOKEN_ROW):
            for iota in range(5):
                start = (first_row + i) * HALF + iota * 16
                tiles[h, start : start + 16, :] = spread[
                    pl.ds(i * HALF + iota, 16, stride=5), :
                ].astype(BF16)

    loads[1].wait()
    for a in range(3):
        for at, rho in enumerate((3, 0, 1, 2)):
            for kappa in range(4):
                start = a * 256 + at * 64 + kappa * 16
                for p in range(2):
                    for q in range(2):
                        b, e = rho - p, kappa - q
                        spot = (slice(start, start + 16), slice((2 * p + q) * C, (2 * p + q + 1) * C))
                        if 0 <= b <= 2 and 0 <= e <= 2:
                            tap = ((a * 3 + b) * 3 + e) * 16
                            w_first[spot] = w_in[tap : tap + 16, :]
                        else:
                            w_first[spot] = jnp.zeros((16, C), BF16)

    loads[2].wait()
    met = (((0,), (1, 2)), ((0, 1), (2,)))
    for p in range(2):
        for q in range(2):
            for i in range(2):
                for j in range(2):
                    total = None
                    for b in met[p][i]:
                        for e in met[q][j]:
                            tap = (b * 3 + e) * C
                            term = w_up[:, tap : tap + C].astype(F32)
                            total = term if total is None else total + term
                    w_phase[2 * p + q, :, (2 * i + j) * C : (2 * i + j + 1) * C] = total.astype(BF16)

    stores = [
        pltpu.make_async_copy(source, target, store_sem.at[n])
        for n, (source, target) in enumerate(((m0, m0_hbm), (m1, m1_hbm), (w_phase, w_phase_hbm)))
    ]
    stores[2].start()
    loads[4].wait()

    def pair_weight(n, carry):
        a, e = n // 3, n % 3
        for part in range(3):
            rows_of = [
                w_mid[pl.ds(pl.multiple_of(((a * 3 + b) * 3 + e) * C + part * 128, 128), 128), :].astype(F32)
                for b in range(3)
            ]
            outer = 0.5 * (rows_of[0] + rows_of[2])
            inner = 0.5 * rows_of[1]
            spot = pl.ds(pl.multiple_of((a * 3 + e) * C + part * 128, 128), 128)
            w_pair[0, spot, :] = (outer + inner).astype(BF16)
            w_pair[1, spot, :] = (outer - inner).astype(BF16)
        return carry

    lax.fori_loop(0, 9, pair_weight, 0)

    top = jnp.where(r == 0, 0.0, 1.0)
    bottom = jnp.where(r == rows - 1, 0.0, 1.0)

    lower = lax.broadcasted_iota(jnp.int32, (5 * HALF, 128), 1) < 64
    def arrive(frames_back):
        for n, (k, d) in enumerate(peers()):
            if k not in frames_back:
                continue

            @pl.when(source_ok(k, d))
            def _(n=n, k=k, d=d):
                copy(n, k, d).wait_recv()

            dst = own.at[k - 1] if d == 0 else above.at[k] if d == 1 else below.at[k]
            unfold(dst[...], BACK - k, 2 if d == 0 else 0 if d == 1 else 5)
        for k in frames_back:
            h = BACK - k
            z[h, :, :128] = jnp.where(lower, tiles[h, 2 * HALF :, :], tiles[h, : 5 * HALF, :])
            z[h, :, 128:] = tiles[h, HALF : 6 * HALF, :]

    loads[0].wait()
    unfold(mine[...], BACK, 2)

    loads[3].wait()
    half_gain = 0.5 * gain[...]
    at = lax.broadcasted_iota(jnp.int32, (16, C), 0)

    def shifted_right(values):
        return jnp.where(at == 0, 0.0, pltpu.roll(values, 1, 0)).astype(BF16)

    def shifted_left(values):
        return jnp.where(at == 15, 0.0, pltpu.roll(values, 15, 0)).astype(BF16)

    def put(target, spot, q, iota, value):
        start = (iota + q) * 16
        target[(*spot, slice(start, start + 16), slice(None))] = value.astype(BF16)
        if q == 0 and iota == 0:
            target[(*spot, slice(80, 96), slice(None))] = shifted_left(value)
        if q == 1 and iota == 4:
            target[(*spot, slice(0, 16), slice(None))] = shifted_right(value)

    def convolve(g, result):
        block = jnp.concatenate([z[g], z[g + 1], z[g + 2]], axis=1)
        for p in range(2):
            part = slice(2 * p * C, 2 * (p + 1) * C)
            result[:, part] = jnp.dot(block, w_first[:, part], preferred_element_type=F32)

    def normed(g, result, q, iota, row):
        w, p = row // 2, row % 2
        rounded = result[
            w * HALF + iota * 16 : w * HALF + (iota + 1) * 16, (2 * p + q) * C : (2 * p + q + 1) * C
        ].astype(BF16)
        if g == 2:
            first[q, row, iota * 16 : (iota + 1) * 16, :] = rounded
        value = rounded.astype(F32)
        scale = lax.rsqrt(jnp.mean(value * value, axis=-1, keepdims=True) + 1e-6)
        if row < 2:
            scale = scale * top
        if row >= 8:
            scale = scale * bottom
        value = value * scale * half_gain
        return value + value * jnp.tanh(value)

    def normalize(g, result):
        for q, target in enumerate((n0, n1)):
            for iota in range(5):
                even = normed(g, result, q, iota, 0)
                odd = normed(g, result, q, iota, 1)
                for pair in range(4):
                    next_even = normed(g, result, q, iota, 2 * pair + 2)
                    next_odd = normed(g, result, q, iota, 2 * pair + 3)
                    put(target, (g, 0, pair), q, iota, even - next_even)
                    put(target, (g, 1, pair), q, iota, odd + next_even)
                    put(target, (g, 2, pair), q, iota, next_even - odd)
                    put(target, (g, 3, pair), q, iota, odd - next_odd)
                    even, odd = next_even, next_odd

    arrive((0, 1, 2))
    convolve(2, result_a)
    arrive((3,))
    convolve(1, result_b)
    normalize(2, result_a)
    arrive((4,))
    convolve(0, result_a)
    normalize(1, result_b)
    normalize(0, result_a)

    def taken(views):
        return jnp.concatenate([view.reshape(4 * HALF, C) for view in views], axis=1)

    for k in range(4):

        def tap(a, e, k=k):
            if k == 0 or k == 3:
                start = ((a * 3 + 2 * (k // 3)) * 3 + e) * C
                return w_mid[start : start + C, :]
            start = (a * 3 + e) * C
            return w_pair[k - 1, start : start + C, :]

        weight = jnp.concatenate(
            [
                jnp.concatenate([tap(a, 1 + i), tap(a, i)], axis=1)
                for a in range(3)
                for i in range(2)
            ],
            axis=0,
        )
        views = [v for a in range(3) for v in (n0[a, k, :, :80, :], n1[a, k, :, 16:, :])]
        both = jnp.dot(taken(views), weight, preferred_element_type=F32)
        for q in range(2):
            weight = jnp.concatenate([tap(a, 2 * q) for a in range(3)], axis=0)
            views = [n0[a, k, :, 16:, :] if q == 1 else n1[a, k, :, :80, :] for a in range(3)]
            value = both[:, q * C : (q + 1) * C] + jnp.dot(
                taken(views), weight, preferred_element_type=F32
            )
            if k == 0:
                sums[0, q] = value
            elif k == 1:
                sums[0, q] += value
                sums[1, q] = value
            elif k == 2:
                sums[0, q] += value
                sums[1, q] -= value
            else:
                sums[1, q] -= value

    for q, target in enumerate((m0, m1)):
        for row in range(8):
            for iota in range(5):
                spot = slice((row // 2) * HALF + iota * 16, (row // 2) * HALF + (iota + 1) * 16)
                value = sums[row % 2, q, spot, :] + first[
                    q, row + 1, iota * 16 : (iota + 1) * 16, :
                ].astype(F32)
                if row == 0:
                    value = value * top
                if row == 7:
                    value = value * bottom
                put(target, (row,), q, iota, value)
        stores[q].start()

    for n, (k, d) in enumerate(peers()):

        @pl.when(target_ok(k, d))
        def _(n=n, k=k, d=d):
            copy(n, k, d).wait_send()
    for store in stores:
        store.wait()


def upsample_kernel(
    m0_hbm, m1_hbm, w_phase_hbm, o_ref, m0, m1, w_phase, turned, out, sems, load_sem
):
    loads = [
        pltpu.make_async_copy(m0_hbm, m0, load_sem.at[4]),
        pltpu.make_async_copy(m1_hbm, m1, load_sem.at[5]),
    ]
    phase_loads = [
        pltpu.make_async_copy(w_phase_hbm.at[n], w_phase.at[n], load_sem.at[n]) for n in range(4)
    ]
    for load in loads + phase_loads:
        load.start()
    for load in loads:
        load.wait()

    def piece(group, n):
        first_iota, count = group
        lanes = pl.ds(pl.multiple_of((n * 30 + first_iota * 6) * 128, 128), count * 6 * 128)
        sem = sems.at[n + (0 if first_iota == 0 else 16)]
        return pltpu.make_async_copy(out.at[:, :, lanes], o_ref.at[:, :, lanes], sem)

    groups = ((0, 3), (3, 2))
    for group in groups:
        first_iota, count = group
        size = count * 16
        plain = slice(first_iota * 16, first_iota * 16 + size)
        after = slice(first_iota * 16 + 16, first_iota * 16 + 16 + size)
        columns = (
            ((m1, plain), (m0, plain), (m1, after)),
            ((m0, plain), (m1, after), (m0, after)),
        )
        for q in range(2):
            for p in range(2):
                halves = []
                for v in range(2):
                    if first_iota == 0 and q == 0:
                        phase_loads[2 * p + v].wait()
                    taken = jnp.concatenate(
                        [
                            source[p + i : p + i + 6, spot, :].reshape(6 * size, C)
                            for i in range(2)
                            for source, spot in columns[q][v : v + 2]
                        ],
                        axis=1,
                    )
                    halves.append(dot_t(taken, w_phase[2 * p + v]))
                whole = jnp.concatenate(halves, axis=1)
                for i in range(6):
                    for at in range(count):
                        for t in range(3):
                            start = ((first_iota + at) * 6 + q * 3 + t) * 16 + 2 * i + p
                            turned[pl.ds(start, 16, stride=480), :] = whole[
                                i * size + at * 16 : i * size + (at + 1) * 16, t * 128 : (t + 1) * 128
                            ]

        def write(n, carry, group=group):
            first_iota, count = group
            for t in range(count * 6):
                tile = n * 30 + first_iota * 6 + t
                out[0, :, pl.ds(pl.multiple_of(tile * 128, 128), 128)] = turned[
                    pl.ds(pl.multiple_of(tile * 16, 16), 12), :
                ].astype(BF16)
            piece(group, n).start()
            return carry

        lax.fori_loop(0, 16, write, 0)

    for group in groups:

        def finish(n, carry, group=group):
            piece(group, n).wait()
            return carry

        lax.fori_loop(0, 16, finish, 0)


def upsample(m0, m1, w_phase):
    return pl.pallas_call(
        upsample_kernel,
        out_shape=jax.ShapeDtypeStruct((1, 12, 2 * 160 * C_UP), BF16),
        in_specs=[pl.BlockSpec(memory_space=pl.ANY)] * 3,
        out_specs=pl.BlockSpec(memory_space=pl.ANY),
        scratch_shapes=[
            *[pltpu.VMEM((8, 96, C), BF16)] * 2,
            pltpu.VMEM((4, C_UP, 4 * C), BF16),
            pltpu.VMEM((160 * 3 * 16, 128), F32),
            pltpu.VMEM((1, 12, 2 * 160 * C_UP), BF16),
            pltpu.SemaphoreType.DMA((32,)),
            pltpu.SemaphoreType.DMA((6,)),
        ],
        compiler_params=pltpu.CompilerParams(vmem_limit_bytes=UP_LIMIT * 2**20),
        name="upsample",
    )(m0, m1, w_phase)


def on_device(frames, rows, latents, conv_in_weight, gain, conv_mid_weight, up_weight):
    n = len(peers())
    m0, m1, w_phase = pl.pallas_call(
        functools.partial(mix_kernel, frames, rows),
        out_shape=[
            jax.ShapeDtypeStruct((8, 96, C), BF16),
            jax.ShapeDtypeStruct((8, 96, C), BF16),
            jax.ShapeDtypeStruct((4, C_UP, 4 * C), BF16),
        ],
        in_specs=[pl.BlockSpec(memory_space=pl.ANY)] * 5,
        out_specs=[pl.BlockSpec(memory_space=pl.ANY)] * 3,
        scratch_shapes=[
            pltpu.VMEM((3 * TOKEN_ROW, 128), BF16),
            pltpu.VMEM((432, C), BF16),
            pltpu.VMEM((1, C), F32),
            pltpu.VMEM((27 * C, C), BF16),
            pltpu.VMEM((C_UP, 9 * C), BF16),
            pltpu.VMEM((768, 4 * C), BF16),
            pltpu.VMEM((4, C_UP, 4 * C), BF16),
            pltpu.VMEM((2, 9 * C, C), BF16),
            *[pltpu.VMEM((8, 96, C), BF16)] * 2,
            pltpu.VMEM((BACK, 3 * TOKEN_ROW, 128), BF16),
            pltpu.VMEM((BACK + 1, 2 * TOKEN_ROW, 128), BF16),
            pltpu.VMEM((BACK + 1, 2 * TOKEN_ROW, 128), BF16),
            pltpu.VMEM((6 * TOKEN_ROW, 128), F32),
            pltpu.VMEM((BACK + 1, 7 * HALF, 128), BF16),
            pltpu.VMEM((BACK + 1, 5 * HALF, 256), BF16),
            pltpu.VMEM((2, 10, HALF, C), BF16),
            *[pltpu.VMEM((3, 4, 4, 96, C), BF16)] * 2,
            *[pltpu.VMEM((5 * HALF, 4 * C), F32)] * 2,
            pltpu.VMEM((2, 2, 4 * HALF, C), F32),
            pltpu.SemaphoreType.DMA((n,)),
            pltpu.SemaphoreType.DMA((n,)),
            pltpu.SemaphoreType.DMA((5,)),
            pltpu.SemaphoreType.DMA((3,)),
        ],
        compiler_params=pltpu.CompilerParams(
            collective_id=0, has_side_effects=True, vmem_limit_bytes=MIX_LIMIT * 2**20
        ),
        name="mix",
    )(latents, conv_in_weight, gain, conv_mid_weight, up_weight.T)
    return upsample(m0, m1, w_phase)


def solution(mesh):
    in_specs = (P(("frames", "rows"), None), P(), P(), P(), P())
    out_specs = P("frames", "rows", None)
    return jax.shard_map(
        functools.partial(on_device, mesh.shape["frames"], mesh.shape["rows"]),
        mesh=mesh,
        in_specs=in_specs,
        out_specs=out_specs,
        check_vma=False,
    )
```

```python
import functools

import jax
import jax.numpy as jnp
from jax import lax
from jax.experimental import pallas as pl
from jax.experimental.pallas import tpu as pltpu
from jax.sharding import PartitionSpec as P

F32 = jnp.float32
BF16 = jnp.bfloat16
MESH = pl.DeviceIdType.MESH
C = 384
C_UP = 192
BACK = 4
HALF = 80
PITCH = 481
MIX_LIMIT, UP_LIMIT = 58, 58
TOKEN_ROW = 40


def peers():
    return [(k, d) for k in range(BACK + 1) for d in (-1, 0, 1) if (k, d) != (0, 0)]


def dot_t(left, right):
    return lax.dot_general(left, right, (((1,), (1,)), ((), ())), preferred_element_type=F32)


def mix_kernel(
    frames, rows,
    x_ref, w_in_hbm, gain_hbm, w_mid_hbm, w_up_hbm,
    m0_hbm, m1_hbm, w_phase_hbm,
    mine, w_in, gain, w_mid, w_up, w_first, w_phase, w_pair, m0, m1,
    own, above, below, spread, tiles, z, first, n0, n1, result_a, result_b, sums,
    send_sem, recv_sem, load_sem, store_sem,
):
    f, r = lax.axis_index("frames"), lax.axis_index("rows")

    def target_ok(k, d):
        return (f + k < frames) & (r + d >= 0) & (r + d < rows)

    def source_ok(k, d):
        return (f - k >= 0) & (r - d >= 0) & (r - d < rows)

    loads = [
        pltpu.make_async_copy(source, target, load_sem.at[n])
        for n, (source, target) in enumerate(
            (
                (x_ref, mine),
                (w_in_hbm, w_in),
                (w_up_hbm, w_up),
                (gain_hbm, gain.at[0]),
                (w_mid_hbm, w_mid),
            )
        )
    ]
    for load in loads:
        load.start()
    barrier = pltpu.get_barrier_semaphore()
    for k, d in peers():

        @pl.when(source_ok(k, d))
        def _(k=k, d=d):
            pl.semaphore_signal(barrier, inc=1, device_id=(f - k, r - d), device_id_type=MESH)

    lane = lax.broadcasted_iota(jnp.int32, (128, 512), 0)
    spot = lax.broadcasted_iota(jnp.int32, (128, 512), 1)
    column = 2 * (lane // 64) + (lane // 16) % 2
    window = (spot // 16) % 4 - column
    part = spot // 128
    wanted = jnp.where(part == 0, 1, jnp.where(part == 1, -1, jnp.where(part == 2, -3, 3)))
    same = ((lane // 32) % 2 == (spot // 64) % 2) & (lane % 16 == spot % 16)
    select = jnp.where(same & (window == wanted), 1.0, 0.0).astype(BF16)

    for k, d in peers():
        dst = own.at[k - 1] if d == 0 else above.at[k] if d == 1 else below.at[k]

        @pl.when(jnp.logical_not(source_ok(k, d)))
        def _(dst=dst):
            dst[...] = jnp.zeros_like(dst)

    loads[1].wait()
    for a in range(3):
        for at, rho in enumerate((3, 0, 1, 2)):
            for kappa in range(4):
                start = a * 256 + at * 64 + kappa * 16
                for p in range(2):
                    for q in range(2):
                        b, e = rho - p, kappa - q
                        spot = (slice(start, start + 16), slice((2 * p + q) * C, (2 * p + q + 1) * C))
                        if 0 <= b <= 2 and 0 <= e <= 2:
                            tap = ((a * 3 + b) * 3 + e) * 16
                            w_first[spot] = w_in[tap : tap + 16, :]
                        else:
                            w_first[spot] = jnp.zeros((16, C), BF16)

    loads[2].wait()
    met = (((0,), (1, 2)), ((0, 1), (2,)))
    for p in range(2):
        for q in range(2):
            for i in range(2):
                for j in range(2):
                    total = None
                    for b in met[p][i]:
                        for e in met[q][j]:
                            tap = (b * 3 + e) * C
                            term = w_up[:, tap : tap + C].astype(F32)
                            total = term if total is None else total + term
                    w_phase[2 * p + q, :, (2 * i + j) * C : (2 * i + j + 1) * C] = total.astype(BF16)

    stores = [
        pltpu.make_async_copy(source, target, store_sem.at[n])
        for n, (source, target) in enumerate(((m0, m0_hbm), (m1, m1_hbm), (w_phase, w_phase_hbm)))
    ]
    stores[2].start()

    def as_int(flag):
        return jnp.where(flag, 1, 0)

    sides = 1 + as_int(r > 0) + as_int(r < rows - 1)
    later = 1 + jnp.minimum(frames - 1 - f, BACK)
    pl.semaphore_wait(barrier, sides * later - 1)

    def copy(n, k, d):
        if d == 0:
            src, dst = x_ref, own.at[k - 1]
        elif d == 1:
            src, dst = x_ref.at[TOKEN_ROW:], above.at[k]
        else:
            src, dst = x_ref.at[: 2 * TOKEN_ROW], below.at[k]
        return pltpu.make_async_remote_copy(
            src_ref=src,
            dst_ref=dst,
            send_sem=send_sem.at[n],
            recv_sem=recv_sem.at[n],
            device_id=(f + k, r + d),
            device_id_type=MESH,
        )

    for n, (k, d) in enumerate(peers()):

        @pl.when(target_ok(k, d))
        def _(n=n, k=k, d=d):
            copy(n, k, d).start()

    def unfold(block, h, first_row):
        count = block.shape[0]
        got = jnp.dot(block, select, preferred_element_type=F32)
        at = lax.broadcasted_iota(jnp.int32, (count, 128), 0) % TOKEN_ROW
        left = jnp.where(at == 0, 0.0, pltpu.roll(got[:, 256:384], 1, 0))
        right = jnp.where(at == TOKEN_ROW - 1, 0.0, pltpu.roll(got[:, 384:], count - 1, 0))
        spread[pl.ds(0, count, stride=2), :] = got[:, :128] + left
        spread[pl.ds(1, count, stride=2), :] = got[:, 128:256] + right
        for i in range(count // TOKEN_ROW):
            for iota in range(5):
                start = (first_row + i) * HALF + iota * 16
                tiles[h, start : start + 16, :] = spread[
                    pl.ds(i * HALF + iota, 16, stride=5), :
                ].astype(BF16)

    loads[4].wait()

    def pair_weight(n, carry):
        a, e = n // 3, n % 3
        for part in range(3):
            rows_of = [
                w_mid[pl.ds(pl.multiple_of(((a * 3 + b) * 3 + e) * C + part * 128, 128), 128), :].astype(F32)
                for b in range(3)
            ]
            outer = 0.5 * (rows_of[0] + rows_of[2])
            inner = 0.5 * rows_of[1]
            spot = pl.ds(pl.multiple_of((a * 3 + e) * C + part * 128, 128), 128)
            w_pair[0, spot, :] = (outer + inner).astype(BF16)
            w_pair[1, spot, :] = (outer - inner).astype(BF16)
        return carry

    lax.fori_loop(0, 9, pair_weight, 0)

    top = jnp.where(r == 0, 0.0, 1.0)
    bottom = jnp.where(r == rows - 1, 0.0, 1.0)

    lower = lax.broadcasted_iota(jnp.int32, (5 * HALF, 128), 1) < 64
    def arrive(frames_back):
        for n, (k, d) in enumerate(peers()):
            if k not in frames_back:
                continue

            @pl.when(source_ok(k, d))
            def _(n=n, k=k, d=d):
                copy(n, k, d).wait_recv()

            dst = own.at[k - 1] if d == 0 else above.at[k] if d == 1 else below.at[k]
            unfold(dst[...], BACK - k, 2 if d == 0 else 0 if d == 1 else 5)
        for k in frames_back:
            h = BACK - k
            z[h, :, :128] = jnp.where(lower, tiles[h, 2 * HALF :, :], tiles[h, : 5 * HALF, :])
            z[h, :, 128:] = tiles[h, HALF : 6 * HALF, :]

    loads[0].wait()
    unfold(mine[...], BACK, 2)

    loads[3].wait()
    half_gain = 0.5 * gain[...]
    at = lax.broadcasted_iota(jnp.int32, (16, C), 0)

    def shifted_right(values):
        return jnp.where(at == 0, 0.0, pltpu.roll(values, 1, 0)).astype(BF16)

    def shifted_left(values):
        return jnp.where(at == 15, 0.0, pltpu.roll(values, 15, 0)).astype(BF16)

    def put(target, spot, q, iota, value):
        start = (iota + q) * 16
        target[(*spot, slice(start, start + 16), slice(None))] = value.astype(BF16)
        if q == 0 and iota == 0:
            target[(*spot, slice(80, 96), slice(None))] = shifted_left(value)
        if q == 1 and iota == 4:
            target[(*spot, slice(0, 16), slice(None))] = shifted_right(value)

    def convolve(g, result):
        block = jnp.concatenate([z[g], z[g + 1], z[g + 2]], axis=1)
        for p in range(2):
            part = slice(2 * p * C, 2 * (p + 1) * C)
            result[:, part] = jnp.dot(block, w_first[:, part], preferred_element_type=F32)

    def normed(g, result, q, iota, row):
        w, p = row // 2, row % 2
        rounded = result[
            w * HALF + iota * 16 : w * HALF + (iota + 1) * 16, (2 * p + q) * C : (2 * p + q + 1) * C
        ].astype(BF16)
        if g == 2:
            first[q, row, iota * 16 : (iota + 1) * 16, :] = rounded
        value = rounded.astype(F32)
        scale = lax.rsqrt(jnp.mean(value * value, axis=-1, keepdims=True) + 1e-6)
        if row < 2:
            scale = scale * top
        if row >= 8:
            scale = scale * bottom
        value = value * scale * half_gain
        return value + value * jnp.tanh(value)

    def normalize(g, result):
        for q, target in enumerate((n0, n1)):
            for iota in range(5):
                even = normed(g, result, q, iota, 0)
                odd = normed(g, result, q, iota, 1)
                for pair in range(4):
                    next_even = normed(g, result, q, iota, 2 * pair + 2)
                    next_odd = normed(g, result, q, iota, 2 * pair + 3)
                    put(target, (g, 0, pair), q, iota, even - next_even)
                    put(target, (g, 1, pair), q, iota, odd + next_even)
                    put(target, (g, 2, pair), q, iota, next_even - odd)
                    put(target, (g, 3, pair), q, iota, odd - next_odd)
                    even, odd = next_even, next_odd

    arrive((0, 1, 2))
    convolve(2, result_a)
    arrive((3,))
    convolve(1, result_b)
    normalize(2, result_a)
    arrive((4,))
    convolve(0, result_a)
    normalize(1, result_b)
    normalize(0, result_a)

    def taken(views):
        return jnp.concatenate([view.reshape(4 * HALF, C) for view in views], axis=1)

    for k in range(4):

        def tap(a, e, k=k):
            if k == 0 or k == 3:
                start = ((a * 3 + 2 * (k // 3)) * 3 + e) * C
                return w_mid[start : start + C, :]
            start = (a * 3 + e) * C
            return w_pair[k - 1, start : start + C, :]

        weight = jnp.concatenate(
            [
                jnp.concatenate([tap(a, 1 + i), tap(a, i)], axis=1)
                for a in range(3)
                for i in range(2)
            ],
            axis=0,
        )
        views = [v for a in range(3) for v in (n0[a, k, :, :80, :], n1[a, k, :, 16:, :])]
        both = jnp.dot(taken(views), weight, preferred_element_type=F32)
        for q in range(2):
            weight = jnp.concatenate([tap(a, 2 * q) for a in range(3)], axis=0)
            views = [n0[a, k, :, 16:, :] if q == 1 else n1[a, k, :, :80, :] for a in range(3)]
            value = both[:, q * C : (q + 1) * C] + jnp.dot(
                taken(views), weight, preferred_element_type=F32
            )
            if k == 0:
                sums[0, q] = value
            elif k == 1:
                sums[0, q] += value
                sums[1, q] = value
            elif k == 2:
                sums[0, q] += value
                sums[1, q] -= value
            else:
                sums[1, q] -= value

    for q, target in enumerate((m0, m1)):
        for row in range(8):
            for iota in range(5):
                spot = slice((row // 2) * HALF + iota * 16, (row // 2) * HALF + (iota + 1) * 16)
                value = sums[row % 2, q, spot, :] + first[
                    q, row + 1, iota * 16 : (iota + 1) * 16, :
                ].astype(F32)
                if row == 0:
                    value = value * top
                if row == 7:
                    value = value * bottom
                put(target, (row,), q, iota, value)
        stores[q].start()

    for n, (k, d) in enumerate(peers()):

        @pl.when(target_ok(k, d))
        def _(n=n, k=k, d=d):
            copy(n, k, d).wait_send()
    for store in stores:
        store.wait()


def upsample_kernel(
    m0_hbm, m1_hbm, w_phase_hbm, o_ref, m0, m1, w_phase, turned, out, sems, load_sem
):
    loads = [
        pltpu.make_async_copy(m0_hbm, m0, load_sem.at[4]),
        pltpu.make_async_copy(m1_hbm, m1, load_sem.at[5]),
    ]
    phase_loads = [
        pltpu.make_async_copy(w_phase_hbm.at[n], w_phase.at[n], load_sem.at[n]) for n in range(4)
    ]
    for load in loads + phase_loads:
        load.start()
    for load in loads:
        load.wait()

    def piece(group, n):
        first_iota, count = group
        lanes = pl.ds(pl.multiple_of((n * 30 + first_iota * 6) * 128, 128), count * 6 * 128)
        sem = sems.at[n + (0 if first_iota == 0 else 16)]
        return pltpu.make_async_copy(out.at[:, :, lanes], o_ref.at[:, :, lanes], sem)

    groups = ((0, 3), (3, 2))
    for group in groups:
        first_iota, count = group
        size = count * 16
        plain = slice(first_iota * 16, first_iota * 16 + size)
        after = slice(first_iota * 16 + 16, first_iota * 16 + 16 + size)
        columns = (
            ((m1, plain), (m0, plain), (m1, after)),
            ((m0, plain), (m1, after), (m0, after)),
        )
        for q in range(2):
            for p in range(2):
                halves = []
                for v in range(2):
                    if first_iota == 0 and q == 0:
                        phase_loads[2 * p + v].wait()
                    taken = jnp.concatenate(
                        [
                            source[p + i : p + i + 6, spot, :].reshape(6 * size, C)
                            for i in range(2)
                            for source, spot in columns[q][v : v + 2]
                        ],
                        axis=1,
                    )
                    halves.append(dot_t(taken, w_phase[2 * p + v]))
                whole = jnp.concatenate(halves, axis=1)
                for i in range(6):
                    for at in range(count):
                        for t in range(3):
                            start = ((first_iota + at) * 6 + q * 3 + t) * 16 + 2 * i + p
                            turned[pl.ds(start, 16, stride=PITCH), :] = whole[
                                i * size + at * 16 : i * size + (at + 1) * 16, t * 128 : (t + 1) * 128
                            ]

        def write(n, carry, group=group):
            first_iota, count = group
            for t in range(count * 6):
                tile = n * 30 + first_iota * 6 + t
                out[0, :, pl.ds(pl.multiple_of(tile * 128, 128), 128)] = turned[
                    pl.ds(n * PITCH + (first_iota * 6 + t) * 16, 12), :
                ].astype(BF16)
            piece(group, n).start()
            return carry

        lax.fori_loop(0, 16, write, 0)

    for group in groups:

        def finish(n, carry, group=group):
            piece(group, n).wait()
            return carry

        lax.fori_loop(0, 16, finish, 0)


def upsample(m0, m1, w_phase):
    return pl.pallas_call(
        upsample_kernel,
        out_shape=jax.ShapeDtypeStruct((1, 12, 2 * 160 * C_UP), BF16),
        in_specs=[pl.BlockSpec(memory_space=pl.ANY)] * 3,
        out_specs=pl.BlockSpec(memory_space=pl.ANY),
        scratch_shapes=[
            *[pltpu.VMEM((8, 96, C), BF16)] * 2,
            pltpu.VMEM((4, C_UP, 4 * C), BF16),
            pltpu.VMEM((16 * PITCH, 128), F32),
            pltpu.VMEM((1, 12, 2 * 160 * C_UP), BF16),
            pltpu.SemaphoreType.DMA((32,)),
            pltpu.SemaphoreType.DMA((6,)),
        ],
        compiler_params=pltpu.CompilerParams(vmem_limit_bytes=UP_LIMIT * 2**20),
        name="upsample",
    )(m0, m1, w_phase)


def on_device(frames, rows, latents, conv_in_weight, gain, conv_mid_weight, up_weight):
    n = len(peers())
    m0, m1, w_phase = pl.pallas_call(
        functools.partial(mix_kernel, frames, rows),
        out_shape=[
            jax.ShapeDtypeStruct((8, 96, C), BF16),
            jax.ShapeDtypeStruct((8, 96, C), BF16),
            jax.ShapeDtypeStruct((4, C_UP, 4 * C), BF16),
        ],
        in_specs=[pl.BlockSpec(memory_space=pl.ANY)] * 5,
        out_specs=[pl.BlockSpec(memory_space=pl.ANY)] * 3,
        scratch_shapes=[
            pltpu.VMEM((3 * TOKEN_ROW, 128), BF16),
            pltpu.VMEM((432, C), BF16),
            pltpu.VMEM((1, C), F32),
            pltpu.VMEM((27 * C, C), BF16),
            pltpu.VMEM((C_UP, 9 * C), BF16),
            pltpu.VMEM((768, 4 * C), BF16),
            pltpu.VMEM((4, C_UP, 4 * C), BF16),
            pltpu.VMEM((2, 9 * C, C), BF16),
            *[pltpu.VMEM((8, 96, C), BF16)] * 2,
            pltpu.VMEM((BACK, 3 * TOKEN_ROW, 128), BF16),
            pltpu.VMEM((BACK + 1, 2 * TOKEN_ROW, 128), BF16),
            pltpu.VMEM((BACK + 1, 2 * TOKEN_ROW, 128), BF16),
            pltpu.VMEM((6 * TOKEN_ROW, 128), F32),
            pltpu.VMEM((BACK + 1, 7 * HALF, 128), BF16),
            pltpu.VMEM((BACK + 1, 5 * HALF, 256), BF16),
            pltpu.VMEM((2, 10, HALF, C), BF16),
            *[pltpu.VMEM((3, 4, 4, 96, C), BF16)] * 2,
            *[pltpu.VMEM((5 * HALF, 4 * C), F32)] * 2,
            pltpu.VMEM((2, 2, 4 * HALF, C), F32),
            pltpu.SemaphoreType.DMA((n,)),
            pltpu.SemaphoreType.DMA((n,)),
            pltpu.SemaphoreType.DMA((5,)),
            pltpu.SemaphoreType.DMA((3,)),
        ],
        compiler_params=pltpu.CompilerParams(
            collective_id=0, has_side_effects=True, vmem_limit_bytes=MIX_LIMIT * 2**20
        ),
        name="mix",
    )(latents, conv_in_weight, gain, conv_mid_weight, up_weight.T)
    return upsample(m0, m1, w_phase)


def solution(mesh):
    in_specs = (P(("frames", "rows"), None), P(), P(), P(), P())
    out_specs = P("frames", "rows", None)
    return jax.shard_map(
        functools.partial(on_device, mesh.shape["frames"], mesh.shape["rows"]),
        mesh=mesh,
        in_specs=in_specs,
        out_specs=out_specs,
        check_vma=False,
    )
```

```python
import functools

import jax
import jax.numpy as jnp
from jax import lax
from jax.experimental import pallas as pl
from jax.experimental.pallas import tpu as pltpu
from jax.sharding import PartitionSpec as P

F32 = jnp.float32
BF16 = jnp.bfloat16
MESH = pl.DeviceIdType.MESH
C = 384
C_UP = 192
BACK = 4
HALF = 80
PITCH = 481
MIX_LIMIT, UP_LIMIT = 58, 58
TOKEN_ROW = 40


def peers():
    return [(k, d) for k in range(BACK + 1) for d in (-1, 0, 1) if (k, d) != (0, 0)]


def dot_t(left, right):
    return lax.dot_general(left, right, (((1,), (1,)), ((), ())), preferred_element_type=F32)


def mix_kernel(
    frames, rows,
    x_ref, w_in_hbm, gain_hbm, w_mid_hbm, w_up_hbm,
    m0_hbm, m1_hbm, w_phase_hbm,
    mine, w_in, gain, w_mid, w_up, w_first, w_phase, w_pair, m0, m1,
    own, above, below, spread, tiles, z, first, n0, n1, result_a, result_b, result_c, sums,
    send_sem, recv_sem, load_sem, store_sem,
):
    f, r = lax.axis_index("frames"), lax.axis_index("rows")

    def target_ok(k, d):
        return (f + k < frames) & (r + d >= 0) & (r + d < rows)

    def source_ok(k, d):
        return (f - k >= 0) & (r - d >= 0) & (r - d < rows)

    loads = [
        pltpu.make_async_copy(source, target, load_sem.at[n])
        for n, (source, target) in enumerate(
            (
                (x_ref, mine),
                (w_in_hbm, w_in),
                (w_up_hbm, w_up),
                (gain_hbm, gain.at[0]),
                (w_mid_hbm, w_mid),
            )
        )
    ]
    for load in loads:
        load.start()
    barrier = pltpu.get_barrier_semaphore()
    for k, d in peers():

        @pl.when(source_ok(k, d))
        def _(k=k, d=d):
            pl.semaphore_signal(barrier, inc=1, device_id=(f - k, r - d), device_id_type=MESH)

    lane = lax.broadcasted_iota(jnp.int32, (128, 512), 0)
    spot = lax.broadcasted_iota(jnp.int32, (128, 512), 1)
    column = 2 * (lane // 64) + (lane // 16) % 2
    window = (spot // 16) % 4 - column
    part = spot // 128
    wanted = jnp.where(part == 0, 1, jnp.where(part == 1, -1, jnp.where(part == 2, -3, 3)))
    same = ((lane // 32) % 2 == (spot // 64) % 2) & (lane % 16 == spot % 16)
    select = jnp.where(same & (window == wanted), 1.0, 0.0).astype(BF16)

    for k, d in peers():
        dst = own.at[k - 1] if d == 0 else above.at[k] if d == 1 else below.at[k]

        @pl.when(jnp.logical_not(source_ok(k, d)))
        def _(dst=dst):
            dst[...] = jnp.zeros_like(dst)

    loads[1].wait()
    for a in range(3):
        for at, rho in enumerate((3, 0, 1, 2)):
            for kappa in range(4):
                start = a * 256 + at * 64 + kappa * 16
                for p in range(2):
                    for q in range(2):
                        b, e = rho - p, kappa - q
                        spot = (slice(start, start + 16), slice((2 * p + q) * C, (2 * p + q + 1) * C))
                        if 0 <= b <= 2 and 0 <= e <= 2:
                            tap = ((a * 3 + b) * 3 + e) * 16
                            w_first[spot] = w_in[tap : tap + 16, :]
                        else:
                            w_first[spot] = jnp.zeros((16, C), BF16)

    loads[2].wait()
    met = (((0,), (1, 2)), ((0, 1), (2,)))
    for p in range(2):
        for q in range(2):
            for i in range(2):
                for j in range(2):
                    total = None
                    for b in met[p][i]:
                        for e in met[q][j]:
                            tap = (b * 3 + e) * C
                            term = w_up[:, tap : tap + C].astype(F32)
                            total = term if total is None else total + term
                    w_phase[2 * p + q, :, (2 * i + j) * C : (2 * i + j + 1) * C] = total.astype(BF16)

    stores = [
        [
            pltpu.make_async_copy(source.at[row], target.at[row], store_sem.at[q * 8 + row])
            for row in range(8)
        ]
        for q, (source, target) in enumerate(((m0, m0_hbm), (m1, m1_hbm)))
    ]
    phase_store = pltpu.make_async_copy(w_phase, w_phase_hbm, store_sem.at[16])
    phase_store.start()

    def as_int(flag):
        return jnp.where(flag, 1, 0)

    sides = 1 + as_int(r > 0) + as_int(r < rows - 1)
    later = 1 + jnp.minimum(frames - 1 - f, BACK)
    pl.semaphore_wait(barrier, sides * later - 1)

    def copy(n, k, d):
        if d == 0:
            src, dst = x_ref, own.at[k - 1]
        elif d == 1:
            src, dst = x_ref.at[TOKEN_ROW:], above.at[k]
        else:
            src, dst = x_ref.at[: 2 * TOKEN_ROW], below.at[k]
        return pltpu.make_async_remote_copy(
            src_ref=src,
            dst_ref=dst,
            send_sem=send_sem.at[n],
            recv_sem=recv_sem.at[n],
            device_id=(f + k, r + d),
            device_id_type=MESH,
        )

    for n, (k, d) in enumerate(peers()):

        @pl.when(target_ok(k, d))
        def _(n=n, k=k, d=d):
            copy(n, k, d).start()

    token = lax.broadcasted_iota(jnp.int32, (7 * TOKEN_ROW, 128), 0) % TOKEN_ROW

    def unfold(k):
        h = BACK - k
        own_band = mine[...] if k == 0 else own[k - 1]
        block = jnp.concatenate([above[k], below[k], own_band], axis=0)
        got = jnp.dot(block, select, preferred_element_type=F32)
        left = jnp.where(token == 0, 0.0, pltpu.roll(got[:, 256:384], 1, 0))
        right = jnp.where(token == TOKEN_ROW - 1, 0.0, pltpu.roll(got[:, 384:], 7 * TOKEN_ROW - 1, 0))
        even, odd = got[:, :128] + left, got[:, 128:256] + right
        for n, row in enumerate((0, 1, 5, 6, 2, 3, 4)):
            part = slice(n * TOKEN_ROW, (n + 1) * TOKEN_ROW)
            start = (h * 7 + row) * HALF
            spread[pl.ds(start, TOKEN_ROW, stride=2), :] = even[part]
            spread[pl.ds(start + 1, TOKEN_ROW, stride=2), :] = odd[part]
        for row in range(7):
            for iota in range(5):
                tiles[h, row * HALF + iota * 16 : row * HALF + (iota + 1) * 16, :] = spread[
                    pl.ds((h * 7 + row) * HALF + iota, 16, stride=5), :
                ].astype(BF16)

    loads[4].wait()

    def pair_weight(n, carry):
        a, e = n // 3, n % 3
        for part in range(3):
            rows_of = [
                w_mid[pl.ds(pl.multiple_of(((a * 3 + b) * 3 + e) * C + part * 128, 128), 128), :].astype(F32)
                for b in range(3)
            ]
            outer = 0.5 * (rows_of[0] + rows_of[2])
            inner = 0.5 * rows_of[1]
            spot = pl.ds(pl.multiple_of((a * 3 + e) * C + part * 128, 128), 128)
            w_pair[0, spot, :] = (outer + inner).astype(BF16)
            w_pair[1, spot, :] = (outer - inner).astype(BF16)
        return carry

    lax.fori_loop(0, 9, pair_weight, 0)

    top = jnp.where(r == 0, 0.0, 1.0)
    bottom = jnp.where(r == rows - 1, 0.0, 1.0)

    lower = lax.broadcasted_iota(jnp.int32, (5 * HALF, 128), 1) < 64
    def arrive(frames_back):
        for n, (k, d) in enumerate(peers()):
            if k in frames_back:

                @pl.when(source_ok(k, d))
                def _(n=n, k=k, d=d):
                    copy(n, k, d).wait_recv()

        for k in frames_back:
            unfold(k)
            h = BACK - k
            z[h, :, :128] = jnp.where(lower, tiles[h, 2 * HALF :, :], tiles[h, : 5 * HALF, :])
            z[h, :, 128:] = tiles[h, HALF : 6 * HALF, :]

    loads[0].wait()
    loads[3].wait()
    half_gain = 0.5 * gain[...]
    at = lax.broadcasted_iota(jnp.int32, (16, C), 0)

    def shifted_right(values):
        return jnp.where(at == 0, 0.0, pltpu.roll(values, 1, 0)).astype(BF16)

    def shifted_left(values):
        return jnp.where(at == 15, 0.0, pltpu.roll(values, 15, 0)).astype(BF16)

    def put(target, spot, q, iota, value):
        start = (iota + q) * 16
        target[(*spot, slice(start, start + 16), slice(None))] = value.astype(BF16)
        if q == 0 and iota == 0:
            target[(*spot, slice(80, 96), slice(None))] = shifted_left(value)
        if q == 1 and iota == 4:
            target[(*spot, slice(0, 16), slice(None))] = shifted_right(value)

    def convolve(g, result):
        block = jnp.concatenate([z[g], z[g + 1], z[g + 2]], axis=1)
        for p in range(2):
            part = slice(2 * p * C, 2 * (p + 1) * C)
            result[:, part] = jnp.dot(block, w_first[:, part], preferred_element_type=F32)

    def normed(g, result, q, iota, row):
        w, p = row // 2, row % 2
        rounded = result[
            w * HALF + iota * 16 : w * HALF + (iota + 1) * 16, (2 * p + q) * C : (2 * p + q + 1) * C
        ].astype(BF16)
        if g == 2:
            first[q, row, iota * 16 : (iota + 1) * 16, :] = rounded
        value = rounded.astype(F32)
        scale = lax.rsqrt(jnp.mean(value * value, axis=-1, keepdims=True) + 1e-6)
        if row < 2:
            scale = scale * top
        if row >= 8:
            scale = scale * bottom
        value = value * scale * half_gain
        return value + value * jnp.tanh(value)

    def normalize(g, result, pieces=range(10)):
        for piece in pieces:
            q, iota = piece // 5, piece % 5
            target = (n0, n1)[q]
            even = normed(g, result, q, iota, 0)
            odd = normed(g, result, q, iota, 1)
            for pair in range(4):
                next_even = normed(g, result, q, iota, 2 * pair + 2)
                next_odd = normed(g, result, q, iota, 2 * pair + 3)
                put(target, (g, 0, pair), q, iota, even - next_even)
                put(target, (g, 1, pair), q, iota, odd + next_even)
                put(target, (g, 2, pair), q, iota, next_even - odd)
                put(target, (g, 3, pair), q, iota, odd - next_odd)
                even, odd = next_even, next_odd

    arrive((0, 1, 2))
    convolve(2, result_a)
    arrive((3,))
    convolve(1, result_b)
    normalize(2, result_a)
    arrive((4,))
    convolve(0, result_c)
    normalize(1, result_b)

    def taken(views):
        return jnp.concatenate([view.reshape(4 * HALF, C) for view in views], axis=1)

    def accumulate(k, frames_of, fresh):
        def tap(a, e):
            if k == 0 or k == 3:
                start = ((a * 3 + 2 * (k // 3)) * 3 + e) * C
                return w_mid[start : start + C, :]
            start = (a * 3 + e) * C
            return w_pair[k - 1, start : start + C, :]

        weight = jnp.concatenate(
            [
                jnp.concatenate([tap(a, 1 + i), tap(a, i)], axis=1)
                for a in frames_of
                for i in range(2)
            ],
            axis=0,
        )
        views = [v for a in frames_of for v in (n0[a, k, :, :80, :], n1[a, k, :, 16:, :])]
        both = jnp.dot(taken(views), weight, preferred_element_type=F32)
        for q in range(2):
            weight = jnp.concatenate([tap(a, 2 * q) for a in frames_of], axis=0)
            views = [n0[a, k, :, 16:, :] if q == 1 else n1[a, k, :, :80, :] for a in frames_of]
            value = both[:, q * C : (q + 1) * C] + jnp.dot(
                taken(views), weight, preferred_element_type=F32
            )
            if k < 3:
                sums[0, q] = value if fresh and k == 0 else sums[0, q] + value
            if k > 0:
                sums[1, q] = value if fresh and k == 1 else sums[1, q] + (value if k == 1 else -value)

    def mix(parity):
        for q, target in enumerate((m0, m1)):
            for pair in range(4):
                row = 2 * pair + parity
                for iota in range(5):
                    spot = slice(pair * HALF + iota * 16, pair * HALF + (iota + 1) * 16)
                    value = sums[parity, q, spot, :] + first[
                        q, row + 1, iota * 16 : (iota + 1) * 16, :
                    ].astype(F32)
                    if row == 0:
                        value = value * top
                    if row == 7:
                        value = value * bottom
                    put(target, (row,), q, iota, value)
                stores[q][row].start()

    for k, pieces in enumerate(((0, 1, 2), (3, 4, 5), (6, 7), (8, 9))):
        accumulate(k, (1, 2), True)
        normalize(0, result_c, pieces)
    for k in range(3):
        accumulate(k, (0,), False)
    mix(0)
    accumulate(3, (0,), False)
    mix(1)

    for n, (k, d) in enumerate(peers()):

        @pl.when(target_ok(k, d))
        def _(n=n, k=k, d=d):
            copy(n, k, d).wait_send()
    for store in stores[0] + stores[1] + [phase_store]:
        store.wait()


def upsample_kernel(
    m0_hbm, m1_hbm, w_phase_hbm, o_ref, m0, m1, w_phase, turned, out, sems, load_sem
):
    loads = [
        pltpu.make_async_copy(m0_hbm, m0, load_sem.at[4]),
        pltpu.make_async_copy(m1_hbm, m1, load_sem.at[5]),
    ]
    phase_loads = [
        pltpu.make_async_copy(w_phase_hbm.at[n], w_phase.at[n], load_sem.at[n]) for n in range(4)
    ]
    for load in loads + phase_loads:
        load.start()
    for load in loads:
        load.wait()

    def piece(group, n):
        first_iota, count = group
        lanes = pl.ds(pl.multiple_of((n * 30 + first_iota * 6) * 128, 128), count * 6 * 128)
        sem = sems.at[n + (0 if first_iota == 0 else 16)]
        return pltpu.make_async_copy(out.at[:, :, lanes], o_ref.at[:, :, lanes], sem)

    groups = ((0, 3), (3, 2))
    for group in groups:
        first_iota, count = group
        size = count * 16
        plain = slice(first_iota * 16, first_iota * 16 + size)
        after = slice(first_iota * 16 + 16, first_iota * 16 + 16 + size)
        columns = (
            ((m1, plain), (m0, plain), (m1, after)),
            ((m0, plain), (m1, after), (m0, after)),
        )
        for q in range(2):
            for p in range(2):
                halves = []
                for v in range(2):
                    if first_iota == 0 and q == 0:
                        phase_loads[2 * p + v].wait()
                    taken = jnp.concatenate(
                        [
                            source[p + i : p + i + 6, spot, :].reshape(6 * size, C)
                            for i in range(2)
                            for source, spot in columns[q][v : v + 2]
                        ],
                        axis=1,
                    )
                    halves.append(dot_t(taken, w_phase[2 * p + v]))
                whole = jnp.concatenate(halves, axis=1)
                for i in range(6):
                    for at in range(count):
                        for t in range(3):
                            start = ((first_iota + at) * 6 + q * 3 + t) * 16 + 2 * i + p
                            turned[pl.ds(start, 16, stride=PITCH), :] = whole[
                                i * size + at * 16 : i * size + (at + 1) * 16, t * 128 : (t + 1) * 128
                            ]

        def write(n, carry, group=group):
            first_iota, count = group
            for t in range(count * 6):
                tile = n * 30 + first_iota * 6 + t
                out[0, :, pl.ds(pl.multiple_of(tile * 128, 128), 128)] = turned[
                    pl.ds(n * PITCH + (first_iota * 6 + t) * 16, 12), :
                ].astype(BF16)
            piece(group, n).start()
            return carry

        lax.fori_loop(0, 16, write, 0)

    for group in groups:

        def finish(n, carry, group=group):
            piece(group, n).wait()
            return carry

        lax.fori_loop(0, 16, finish, 0)


def upsample(m0, m1, w_phase):
    return pl.pallas_call(
        upsample_kernel,
        out_shape=jax.ShapeDtypeStruct((1, 12, 2 * 160 * C_UP), BF16),
        in_specs=[pl.BlockSpec(memory_space=pl.ANY)] * 3,
        out_specs=pl.BlockSpec(memory_space=pl.ANY),
        scratch_shapes=[
            *[pltpu.VMEM((8, 96, C), BF16)] * 2,
            pltpu.VMEM((4, C_UP, 4 * C), BF16),
            pltpu.VMEM((16 * PITCH, 128), F32),
            pltpu.VMEM((1, 12, 2 * 160 * C_UP), BF16),
            pltpu.SemaphoreType.DMA((32,)),
            pltpu.SemaphoreType.DMA((6,)),
        ],
        compiler_params=pltpu.CompilerParams(vmem_limit_bytes=UP_LIMIT * 2**20),
        name="upsample",
    )(m0, m1, w_phase)


def on_device(frames, rows, latents, conv_in_weight, gain, conv_mid_weight, up_weight):
    n = len(peers())
    m0, m1, w_phase = pl.pallas_call(
        functools.partial(mix_kernel, frames, rows),
        out_shape=[
            jax.ShapeDtypeStruct((8, 96, C), BF16),
            jax.ShapeDtypeStruct((8, 96, C), BF16),
            jax.ShapeDtypeStruct((4, C_UP, 4 * C), BF16),
        ],
        in_specs=[pl.BlockSpec(memory_space=pl.ANY)] * 5,
        out_specs=[pl.BlockSpec(memory_space=pl.ANY)] * 3,
        scratch_shapes=[
            pltpu.VMEM((3 * TOKEN_ROW, 128), BF16),
            pltpu.VMEM((432, C), BF16),
            pltpu.VMEM((1, C), F32),
            pltpu.VMEM((27 * C, C), BF16),
            pltpu.VMEM((C_UP, 9 * C), BF16),
            pltpu.VMEM((768, 4 * C), BF16),
            pltpu.VMEM((4, C_UP, 4 * C), BF16),
            pltpu.VMEM((2, 9 * C, C), BF16),
            *[pltpu.VMEM((8, 96, C), BF16)] * 2,
            pltpu.VMEM((BACK, 3 * TOKEN_ROW, 128), BF16),
            pltpu.VMEM((BACK + 1, 2 * TOKEN_ROW, 128), BF16),
            pltpu.VMEM((BACK + 1, 2 * TOKEN_ROW, 128), BF16),
            pltpu.VMEM(((BACK + 1) * 7 * HALF, 128), F32),
            pltpu.VMEM((BACK + 1, 7 * HALF, 128), BF16),
            pltpu.VMEM((BACK + 1, 5 * HALF, 256), BF16),
            pltpu.VMEM((2, 10, HALF, C), BF16),
            *[pltpu.VMEM((3, 4, 4, 96, C), BF16)] * 2,
            *[pltpu.VMEM((5 * HALF, 4 * C), F32)] * 3,
            pltpu.VMEM((2, 2, 4 * HALF, C), F32),
            pltpu.SemaphoreType.DMA((n,)),
            pltpu.SemaphoreType.DMA((n,)),
            pltpu.SemaphoreType.DMA((5,)),
            pltpu.SemaphoreType.DMA((17,)),
        ],
        compiler_params=pltpu.CompilerParams(
            collective_id=0, has_side_effects=True, vmem_limit_bytes=MIX_LIMIT * 2**20
        ),
        name="mix",
    )(latents, conv_in_weight, gain, conv_mid_weight, up_weight.T)
    return upsample(m0, m1, w_phase)


def solution(mesh):
    in_specs = (P(("frames", "rows"), None), P(), P(), P(), P())
    out_specs = P("frames", "rows", None)
    return jax.shard_map(
        functools.partial(on_device, mesh.shape["frames"], mesh.shape["rows"]),
        mesh=mesh,
        in_specs=in_specs,
        out_specs=out_specs,
        check_vma=False,
    )
```

```python
import functools

import jax
import jax.numpy as jnp
from jax import lax
from jax.experimental import pallas as pl
from jax.experimental.pallas import tpu as pltpu
from jax.sharding import PartitionSpec as P

F32 = jnp.float32
BF16 = jnp.bfloat16
MESH = pl.DeviceIdType.MESH
C = 384
C_UP = 192
BACK = 4
HALF = 80
PITCH = 481
MIX_LIMIT, UP_LIMIT = 58, 58
TOKEN_ROW = 40


def peers():
    return [(k, d) for k in range(BACK + 1) for d in (-1, 0, 1) if (k, d) != (0, 0)]


def dot_t(left, right):
    return lax.dot_general(left, right, (((1,), (1,)), ((), ())), preferred_element_type=F32)


def mix_kernel(
    frames, rows,
    x_ref, w_in_hbm, gain_hbm, w_mid_hbm, w_up_hbm,
    m0_hbm, m1_hbm, w_phase_hbm,
    mine, w_in, gain, w_mid, w_up, w_first, w_phase, w_pair, m0, m1,
    own, above, below, spread, tiles, z, first, n0, n1, result_a, result_b, result_c, sums,
    send_sem, recv_sem, load_sem, store_sem,
):
    f, r = lax.axis_index("frames"), lax.axis_index("rows")

    def target_ok(k, d):
        return (f + k < frames) & (r + d >= 0) & (r + d < rows)

    def source_ok(k, d):
        return (f - k >= 0) & (r - d >= 0) & (r - d < rows)

    loads = [
        pltpu.make_async_copy(source, target, load_sem.at[n])
        for n, (source, target) in enumerate(
            (
                (x_ref, mine),
                (w_in_hbm, w_in),
                (w_up_hbm, w_up),
                (gain_hbm, gain.at[0]),
                (w_mid_hbm, w_mid),
            )
        )
    ]
    for load in loads:
        load.start()
    barrier = pltpu.get_barrier_semaphore()
    for k, d in peers():

        @pl.when(source_ok(k, d))
        def _(k=k, d=d):
            pl.semaphore_signal(barrier, inc=1, device_id=(f - k, r - d), device_id_type=MESH)

    lane = lax.broadcasted_iota(jnp.int32, (128, 512), 0)
    spot = lax.broadcasted_iota(jnp.int32, (128, 512), 1)
    column = 2 * (lane // 64) + (lane // 16) % 2
    window = (spot // 16) % 4 - column
    part = spot // 128
    wanted = jnp.where(part == 0, 1, jnp.where(part == 1, -1, jnp.where(part == 2, -3, 3)))
    same = ((lane // 32) % 2 == (spot // 64) % 2) & (lane % 16 == spot % 16)
    select = jnp.where(same & (window == wanted), 1.0, 0.0).astype(BF16)

    for k, d in peers():
        dst = own.at[k - 1] if d == 0 else above.at[k] if d == 1 else below.at[k]

        @pl.when(jnp.logical_not(source_ok(k, d)))
        def _(dst=dst):
            dst[...] = jnp.zeros_like(dst)

    loads[1].wait()
    for a in range(3):
        for at, rho in enumerate((3, 0, 1, 2)):
            for kappa in range(4):
                start = a * 256 + at * 64 + kappa * 16
                for p in range(2):
                    for q in range(2):
                        b, e = rho - p, kappa - q
                        spot = (slice(start, start + 16), slice((2 * p + q) * C, (2 * p + q + 1) * C))
                        if 0 <= b <= 2 and 0 <= e <= 2:
                            tap = ((a * 3 + b) * 3 + e) * 16
                            w_first[spot] = w_in[tap : tap + 16, :]
                        else:
                            w_first[spot] = jnp.zeros((16, C), BF16)

    loads[2].wait()
    met = (((0,), (1, 2)), ((0, 1), (2,)))
    for v in range(2):
        for j in range(2):
            spot = slice(j * C, (j + 1) * C)
            by_row = []
            for b in range(3):
                total = None
                for e in met[v][j]:
                    tap = (b * 3 + e) * C
                    term = w_up[:, tap : tap + C].astype(F32)
                    total = term if total is None else total + term
                by_row.append(total)
            w_phase[v, :, spot] = (by_row[0] + by_row[1] + by_row[2]).astype(BF16)
            w_phase[2 + v, :, spot] = (-by_row[0]).astype(BF16)
            w_phase[4 + v, :, spot] = by_row[2].astype(BF16)

    stores = [
        [
            pltpu.make_async_copy(source.at[row], target.at[row], store_sem.at[q * 8 + row])
            for row in range(8)
        ]
        for q, (source, target) in enumerate(((m0, m0_hbm), (m1, m1_hbm)))
    ]
    phase_store = pltpu.make_async_copy(w_phase, w_phase_hbm, store_sem.at[16])
    phase_store.start()

    def as_int(flag):
        return jnp.where(flag, 1, 0)

    sides = 1 + as_int(r > 0) + as_int(r < rows - 1)
    later = 1 + jnp.minimum(frames - 1 - f, BACK)
    pl.semaphore_wait(barrier, sides * later - 1)

    def copy(n, k, d):
        if d == 0:
            src, dst = x_ref, own.at[k - 1]
        elif d == 1:
            src, dst = x_ref.at[TOKEN_ROW:], above.at[k]
        else:
            src, dst = x_ref.at[: 2 * TOKEN_ROW], below.at[k]
        return pltpu.make_async_remote_copy(
            src_ref=src,
            dst_ref=dst,
            send_sem=send_sem.at[n],
            recv_sem=recv_sem.at[n],
            device_id=(f + k, r + d),
            device_id_type=MESH,
        )

    for n, (k, d) in enumerate(peers()):

        @pl.when(target_ok(k, d))
        def _(n=n, k=k, d=d):
            copy(n, k, d).start()

    token = lax.broadcasted_iota(jnp.int32, (7 * TOKEN_ROW, 128), 0) % TOKEN_ROW

    def unfold(k):
        h = BACK - k
        own_band = mine[...] if k == 0 else own[k - 1]
        block = jnp.concatenate([above[k], below[k], own_band], axis=0)
        got = jnp.dot(block, select, preferred_element_type=F32)
        left = jnp.where(token == 0, 0.0, pltpu.roll(got[:, 256:384], 1, 0))
        right = jnp.where(token == TOKEN_ROW - 1, 0.0, pltpu.roll(got[:, 384:], 7 * TOKEN_ROW - 1, 0))
        even, odd = got[:, :128] + left, got[:, 128:256] + right
        for n, row in enumerate((0, 1, 5, 6, 2, 3, 4)):
            part = slice(n * TOKEN_ROW, (n + 1) * TOKEN_ROW)
            start = (h * 7 + row) * HALF
            spread[pl.ds(start, TOKEN_ROW, stride=2), :] = even[part]
            spread[pl.ds(start + 1, TOKEN_ROW, stride=2), :] = odd[part]
        for row in range(7):
            for iota in range(5):
                tiles[h, row * HALF + iota * 16 : row * HALF + (iota + 1) * 16, :] = spread[
                    pl.ds((h * 7 + row) * HALF + iota, 16, stride=5), :
                ].astype(BF16)

    loads[4].wait()

    def pair_weight(n, carry):
        a, e = n // 3, n % 3
        for part in range(3):
            rows_of = [
                w_mid[pl.ds(pl.multiple_of(((a * 3 + b) * 3 + e) * C + part * 128, 128), 128), :].astype(F32)
                for b in range(3)
            ]
            outer = 0.5 * (rows_of[0] + rows_of[2])
            inner = 0.5 * rows_of[1]
            spot = pl.ds(pl.multiple_of((a * 3 + e) * C + part * 128, 128), 128)
            w_pair[0, spot, :] = (outer + inner).astype(BF16)
            w_pair[1, spot, :] = (outer - inner).astype(BF16)
        return carry

    lax.fori_loop(0, 9, pair_weight, 0)

    top = jnp.where(r == 0, 0.0, 1.0)
    bottom = jnp.where(r == rows - 1, 0.0, 1.0)

    lower = lax.broadcasted_iota(jnp.int32, (5 * HALF, 128), 1) < 64
    def arrive(frames_back):
        for n, (k, d) in enumerate(peers()):
            if k in frames_back:

                @pl.when(source_ok(k, d))
                def _(n=n, k=k, d=d):
                    copy(n, k, d).wait_recv()

        for k in frames_back:
            unfold(k)
            h = BACK - k
            z[h, :, :128] = jnp.where(lower, tiles[h, 2 * HALF :, :], tiles[h, : 5 * HALF, :])
            z[h, :, 128:] = tiles[h, HALF : 6 * HALF, :]

    loads[0].wait()
    loads[3].wait()
    half_gain = 0.5 * gain[...]
    at = lax.broadcasted_iota(jnp.int32, (16, C), 0)

    def shifted_right(values):
        return jnp.where(at == 0, 0.0, pltpu.roll(values, 1, 0)).astype(BF16)

    def shifted_left(values):
        return jnp.where(at == 15, 0.0, pltpu.roll(values, 15, 0)).astype(BF16)

    def put(target, spot, q, iota, value):
        start = (iota + q) * 16
        target[(*spot, slice(start, start + 16), slice(None))] = value.astype(BF16)
        if q == 0 and iota == 0:
            target[(*spot, slice(80, 96), slice(None))] = shifted_left(value)
        if q == 1 and iota == 4:
            target[(*spot, slice(0, 16), slice(None))] = shifted_right(value)

    def convolve(g, result):
        block = jnp.concatenate([z[g], z[g + 1], z[g + 2]], axis=1)
        for p in range(2):
            part = slice(2 * p * C, 2 * (p + 1) * C)
            result[:, part] = jnp.dot(block, w_first[:, part], preferred_element_type=F32)

    def normed(g, result, q, iota, row):
        w, p = row // 2, row % 2
        rounded = result[
            w * HALF + iota * 16 : w * HALF + (iota + 1) * 16, (2 * p + q) * C : (2 * p + q + 1) * C
        ].astype(BF16)
        if g == 2:
            first[q, row, iota * 16 : (iota + 1) * 16, :] = rounded
        value = rounded.astype(F32)
        scale = lax.rsqrt(jnp.mean(value * value, axis=-1, keepdims=True) + 1e-6)
        if row < 2:
            scale = scale * top
        if row >= 8:
            scale = scale * bottom
        value = value * scale * half_gain
        return value + value * jnp.tanh(value)

    def normalize(g, result, pieces=range(10)):
        for piece in pieces:
            q, iota = piece // 5, piece % 5
            target = (n0, n1)[q]
            even = normed(g, result, q, iota, 0)
            odd = normed(g, result, q, iota, 1)
            for pair in range(4):
                next_even = normed(g, result, q, iota, 2 * pair + 2)
                next_odd = normed(g, result, q, iota, 2 * pair + 3)
                put(target, (g, 0, pair), q, iota, even - next_even)
                put(target, (g, 1, pair), q, iota, odd + next_even)
                put(target, (g, 2, pair), q, iota, next_even - odd)
                put(target, (g, 3, pair), q, iota, odd - next_odd)
                even, odd = next_even, next_odd

    arrive((0, 1, 2))
    convolve(2, result_a)
    arrive((3,))
    convolve(1, result_b)
    normalize(2, result_a)
    arrive((4,))
    convolve(0, result_c)
    normalize(1, result_b)

    def taken(views):
        return jnp.concatenate([view.reshape(4 * HALF, C) for view in views], axis=1)

    def accumulate(k, frames_of, fresh):
        def tap(a, e):
            if k == 0 or k == 3:
                start = ((a * 3 + 2 * (k // 3)) * 3 + e) * C
                return w_mid[start : start + C, :]
            start = (a * 3 + e) * C
            return w_pair[k - 1, start : start + C, :]

        weight = jnp.concatenate(
            [
                jnp.concatenate([tap(a, 1 + i), tap(a, i)], axis=1)
                for a in frames_of
                for i in range(2)
            ],
            axis=0,
        )
        views = [v for a in frames_of for v in (n0[a, k, :, :80, :], n1[a, k, :, 16:, :])]
        both = jnp.dot(taken(views), weight, preferred_element_type=F32)
        for q in range(2):
            weight = jnp.concatenate([tap(a, 2 * q) for a in frames_of], axis=0)
            views = [n0[a, k, :, 16:, :] if q == 1 else n1[a, k, :, :80, :] for a in frames_of]
            value = both[:, q * C : (q + 1) * C] + jnp.dot(
                taken(views), weight, preferred_element_type=F32
            )
            if k < 3:
                sums[0, q] = value if fresh and k == 0 else sums[0, q] + value
            if k > 0:
                sums[1, q] = value if fresh and k == 1 else sums[1, q] + (value if k == 1 else -value)

    def mix(parity):
        for q, target in enumerate((m0, m1)):
            for pair in range(4):
                row = 2 * pair + parity
                for iota in range(5):
                    spot = slice(pair * HALF + iota * 16, pair * HALF + (iota + 1) * 16)
                    value = sums[parity, q, spot, :] + first[
                        q, row + 1, iota * 16 : (iota + 1) * 16, :
                    ].astype(F32)
                    if row == 0:
                        value = value * top
                    if row == 7:
                        value = value * bottom
                    put(target, (row,), q, iota, value)
                stores[q][row].start()

    for k, pieces in enumerate(((0, 1, 2), (3, 4, 5), (6, 7), (8, 9))):
        accumulate(k, (1, 2), True)
        normalize(0, result_c, pieces)
    for k in range(3):
        accumulate(k, (0,), False)
    mix(0)
    accumulate(3, (0,), False)
    mix(1)

    for n, (k, d) in enumerate(peers()):

        @pl.when(target_ok(k, d))
        def _(n=n, k=k, d=d):
            copy(n, k, d).wait_send()
    for store in stores[0] + stores[1] + [phase_store]:
        store.wait()


def upsample_kernel(
    m0_hbm, m1_hbm, w_phase_hbm, o_ref, m0, m1, w_phase, d0, d1, turned, out, out_sem, load_sem
):
    loads = [
        pltpu.make_async_copy(m0_hbm, m0, load_sem.at[6]),
        pltpu.make_async_copy(m1_hbm, m1, load_sem.at[7]),
    ]
    phase_loads = [
        pltpu.make_async_copy(w_phase_hbm.at[n], w_phase.at[n], load_sem.at[n]) for n in range(6)
    ]
    for load in loads + phase_loads:
        load.start()
    for load in loads:
        load.wait()
    for difference, source in ((d0, m0), (d1, m1)):
        difference[...] = (source[1:].astype(F32) - source[:7].astype(F32)).astype(BF16)

    def piece(group, n):
        first_iota, count = group
        lanes = pl.ds(pl.multiple_of((n * 30 + first_iota * 6) * 128, 128), count * 6 * 128)
        return pltpu.make_async_copy(out.at[:, :, lanes], o_ref.at[:, :, lanes], out_sem)

    groups = ((0, 3), (3, 2))
    for group in groups:
        first_iota, count = group
        size = count * 16
        plain = slice(first_iota * 16, first_iota * 16 + size)
        after = slice(first_iota * 16 + 16, first_iota * 16 + 16 + size)
        places = (((1, plain), (0, plain), (1, after)), ((0, plain), (1, after), (0, after)))

        def product(pair, row, number, q, v, size=size, places=places):
            taken = jnp.concatenate(
                [
                    pair[parity][row : row + 6, spot, :].reshape(6 * size, C)
                    for parity, spot in places[q][v : v + 2]
                ],
                axis=1,
            )
            if first_iota == 0 and q == 0:
                phase_loads[number].wait()
            return dot_t(taken, w_phase[number])

        for q in range(2):
            centre = [product((m0, m1), 1, v, q, v) for v in range(2)]
            for p in range(2):
                halves = [
                    centre[v] + product((d0, d1), p, 2 + 2 * p + v, q, v) for v in range(2)
                ]
                whole = jnp.concatenate(halves, axis=1)
                for i in range(6):
                    for at in range(count):
                        for t in range(3):
                            start = ((first_iota + at) * 6 + q * 3 + t) * 16 + 2 * i + p
                            turned[pl.ds(start, 16, stride=PITCH), :] = whole[
                                i * size + at * 16 : i * size + (at + 1) * 16, t * 128 : (t + 1) * 128
                            ]

        def write(n, carry, group=group):
            first_iota, count = group
            for t in range(count * 6):
                tile = n * 30 + first_iota * 6 + t
                out[0, :, pl.ds(pl.multiple_of(tile * 128, 128), 128)] = turned[
                    pl.ds(n * PITCH + (first_iota * 6 + t) * 16, 12), :
                ].astype(BF16)
            piece(group, n).start()
            return carry

        lax.fori_loop(0, 16, write, 0)

    pltpu.make_async_copy(out, o_ref, out_sem).wait()


def upsample(m0, m1, w_phase):
    return pl.pallas_call(
        upsample_kernel,
        out_shape=jax.ShapeDtypeStruct((1, 12, 2 * 160 * C_UP), BF16),
        in_specs=[pl.BlockSpec(memory_space=pl.ANY)] * 3,
        out_specs=pl.BlockSpec(memory_space=pl.ANY),
        scratch_shapes=[
            *[pltpu.VMEM((8, 96, C), BF16)] * 2,
            pltpu.VMEM((6, C_UP, 2 * C), BF16),
            *[pltpu.VMEM((7, 96, C), BF16)] * 2,
            pltpu.VMEM((16 * PITCH, 128), F32),
            pltpu.VMEM((1, 12, 2 * 160 * C_UP), BF16),
            pltpu.SemaphoreType.DMA,
            pltpu.SemaphoreType.DMA((8,)),
        ],
        compiler_params=pltpu.CompilerParams(vmem_limit_bytes=UP_LIMIT * 2**20),
        name="upsample",
    )(m0, m1, w_phase)


def on_device(frames, rows, latents, conv_in_weight, gain, conv_mid_weight, up_weight):
    n = len(peers())
    m0, m1, w_phase = pl.pallas_call(
        functools.partial(mix_kernel, frames, rows),
        out_shape=[
            jax.ShapeDtypeStruct((8, 96, C), BF16),
            jax.ShapeDtypeStruct((8, 96, C), BF16),
            jax.ShapeDtypeStruct((6, C_UP, 2 * C), BF16),
        ],
        in_specs=[pl.BlockSpec(memory_space=pl.ANY)] * 5,
        out_specs=[pl.BlockSpec(memory_space=pl.ANY)] * 3,
        scratch_shapes=[
            pltpu.VMEM((3 * TOKEN_ROW, 128), BF16),
            pltpu.VMEM((432, C), BF16),
            pltpu.VMEM((1, C), F32),
            pltpu.VMEM((27 * C, C), BF16),
            pltpu.VMEM((C_UP, 9 * C), BF16),
            pltpu.VMEM((768, 4 * C), BF16),
            pltpu.VMEM((6, C_UP, 2 * C), BF16),
            pltpu.VMEM((2, 9 * C, C), BF16),
            *[pltpu.VMEM((8, 96, C), BF16)] * 2,
            pltpu.VMEM((BACK, 3 * TOKEN_ROW, 128), BF16),
            pltpu.VMEM((BACK + 1, 2 * TOKEN_ROW, 128), BF16),
            pltpu.VMEM((BACK + 1, 2 * TOKEN_ROW, 128), BF16),
            pltpu.VMEM(((BACK + 1) * 7 * HALF, 128), F32),
            pltpu.VMEM((BACK + 1, 7 * HALF, 128), BF16),
            pltpu.VMEM((BACK + 1, 5 * HALF, 256), BF16),
            pltpu.VMEM((2, 10, HALF, C), BF16),
            *[pltpu.VMEM((3, 4, 4, 96, C), BF16)] * 2,
            *[pltpu.VMEM((5 * HALF, 4 * C), F32)] * 3,
            pltpu.VMEM((2, 2, 4 * HALF, C), F32),
            pltpu.SemaphoreType.DMA((n,)),
            pltpu.SemaphoreType.DMA((n,)),
            pltpu.SemaphoreType.DMA((5,)),
            pltpu.SemaphoreType.DMA((17,)),
        ],
        compiler_params=pltpu.CompilerParams(
            collective_id=0, has_side_effects=True, vmem_limit_bytes=MIX_LIMIT * 2**20
        ),
        name="mix",
    )(latents, conv_in_weight, gain, conv_mid_weight, up_weight.T)
    return upsample(m0, m1, w_phase)


def solution(mesh):
    in_specs = (P(("frames", "rows"), None), P(), P(), P(), P())
    out_specs = P("frames", "rows", None)
    return jax.shard_map(
        functools.partial(on_device, mesh.shape["frames"], mesh.shape["rows"]),
        mesh=mesh,
        in_specs=in_specs,
        out_specs=out_specs,
        check_vma=False,
    )
```

```python
import functools

import jax
import jax.numpy as jnp
from jax import lax
from jax.experimental import pallas as pl
from jax.experimental.pallas import tpu as pltpu
from jax.sharding import PartitionSpec as P

F32 = jnp.float32
BF16 = jnp.bfloat16
MESH = pl.DeviceIdType.MESH
C = 384
C_UP = 192
BACK = 4
HALF = 80
PITCH = 481
MIX_LIMIT, UP_LIMIT = 58, 58
TOKEN_ROW = 40


def peers():
    return [(k, d) for k in range(BACK + 1) for d in (-1, 0, 1) if (k, d) != (0, 0)]


def dot_t(left, right):
    return lax.dot_general(left, right, (((1,), (1,)), ((), ())), preferred_element_type=F32)


def mix_kernel(
    frames, rows,
    x_ref, w_in_hbm, gain_hbm, w_mid_hbm, w_up_hbm,
    m0_hbm, m1_hbm, w_phase_hbm,
    mine, w_in, gain, w_mid, w_up, w_first, w_phase, w_pair, m0, m1,
    own, above, below, spread, tiles, z, first, n0, n1, result_a, result_b, result_c, sums,
    send_sem, recv_sem, load_sem, store_sem,
):
    f, r = lax.axis_index("frames"), lax.axis_index("rows")

    def target_ok(k, d):
        return (f + k < frames) & (r + d >= 0) & (r + d < rows)

    def source_ok(k, d):
        return (f - k >= 0) & (r - d >= 0) & (r - d < rows)

    loads = [
        pltpu.make_async_copy(source, target, load_sem.at[n])
        for n, (source, target) in enumerate(
            (
                (x_ref, mine),
                (w_in_hbm, w_in),
                (w_up_hbm, w_up),
                (gain_hbm, gain.at[0]),
                (w_mid_hbm, w_mid),
            )
        )
    ]
    for load in loads:
        load.start()
    barrier = pltpu.get_barrier_semaphore()
    for k, d in peers():

        @pl.when(source_ok(k, d))
        def _(k=k, d=d):
            pl.semaphore_signal(barrier, inc=1, device_id=(f - k, r - d), device_id_type=MESH)

    lane = lax.broadcasted_iota(jnp.int32, (128, 512), 0)
    spot = lax.broadcasted_iota(jnp.int32, (128, 512), 1)
    column = 2 * (lane // 64) + (lane // 16) % 2
    window = (spot // 16) % 4 - column
    part = spot // 128
    wanted = jnp.where(part == 0, 1, jnp.where(part == 1, -1, jnp.where(part == 2, -3, 3)))
    same = ((lane // 32) % 2 == (spot // 64) % 2) & (lane % 16 == spot % 16)
    select = jnp.where(same & (window == wanted), 1.0, 0.0).astype(BF16)

    for k, d in peers():
        dst = own.at[k - 1] if d == 0 else above.at[k] if d == 1 else below.at[k]

        @pl.when(jnp.logical_not(source_ok(k, d)))
        def _(dst=dst):
            dst[...] = jnp.zeros_like(dst)

    loads[1].wait()
    for a in range(3):
        for at, rho in enumerate((3, 0, 1, 2)):
            for kappa in range(4):
                start = a * 256 + at * 64 + kappa * 16
                for p in range(2):
                    for q in range(2):
                        b, e = rho - p, kappa - q
                        spot = (slice(start, start + 16), slice((2 * p + q) * C, (2 * p + q + 1) * C))
                        if 0 <= b <= 2 and 0 <= e <= 2:
                            tap = ((a * 3 + b) * 3 + e) * 16
                            w_first[spot] = w_in[tap : tap + 16, :]
                        else:
                            w_first[spot] = jnp.zeros((16, C), BF16)

    loads[2].wait()
    met = (((0,), (1, 2)), ((0, 1), (2,)))
    for v in range(2):
        for j in range(2):
            spot = slice(j * C, (j + 1) * C)
            by_row = []
            for b in range(3):
                total = None
                for e in met[v][j]:
                    tap = (b * 3 + e) * C
                    term = w_up[:, tap : tap + C].astype(F32)
                    total = term if total is None else total + term
                by_row.append(total)
            w_phase[v, :, spot] = (by_row[0] + by_row[1] + by_row[2]).astype(BF16)
            w_phase[2 + v, :, spot] = (-by_row[0]).astype(BF16)
            w_phase[4 + v, :, spot] = by_row[2].astype(BF16)

    stores = [
        [
            pltpu.make_async_copy(source.at[row], target.at[row], store_sem.at[q * 8 + row])
            for row in range(8)
        ]
        for q, (source, target) in enumerate(((m0, m0_hbm), (m1, m1_hbm)))
    ]
    phase_store = pltpu.make_async_copy(w_phase, w_phase_hbm, store_sem.at[16])
    phase_store.start()

    def as_int(flag):
        return jnp.where(flag, 1, 0)

    sides = 1 + as_int(r > 0) + as_int(r < rows - 1)
    later = 1 + jnp.minimum(frames - 1 - f, BACK)
    pl.semaphore_wait(barrier, sides * later - 1)

    def copy(n, k, d):
        if d == 0:
            src, dst = x_ref, own.at[k - 1]
        elif d == 1:
            src, dst = x_ref.at[TOKEN_ROW:], above.at[k]
        else:
            src, dst = x_ref.at[: 2 * TOKEN_ROW], below.at[k]
        return pltpu.make_async_remote_copy(
            src_ref=src,
            dst_ref=dst,
            send_sem=send_sem.at[n],
            recv_sem=recv_sem.at[n],
            device_id=(f + k, r + d),
            device_id_type=MESH,
        )

    for n, (k, d) in enumerate(peers()):

        @pl.when(target_ok(k, d))
        def _(n=n, k=k, d=d):
            copy(n, k, d).start()

    token = lax.broadcasted_iota(jnp.int32, (7 * TOKEN_ROW, 128), 0) % TOKEN_ROW

    def unfold(k):
        h = BACK - k
        own_band = mine[...] if k == 0 else own[k - 1]
        block = jnp.concatenate([above[k], below[k], own_band], axis=0)
        got = jnp.dot(block, select, preferred_element_type=F32)
        left = jnp.where(token == 0, 0.0, pltpu.roll(got[:, 256:384], 1, 0))
        right = jnp.where(token == TOKEN_ROW - 1, 0.0, pltpu.roll(got[:, 384:], 7 * TOKEN_ROW - 1, 0))
        even, odd = got[:, :128] + left, got[:, 128:256] + right
        for n, row in enumerate((0, 1, 5, 6, 2, 3, 4)):
            part = slice(n * TOKEN_ROW, (n + 1) * TOKEN_ROW)
            start = (h * 7 + row) * HALF
            spread[pl.ds(start, TOKEN_ROW, stride=2), :] = even[part]
            spread[pl.ds(start + 1, TOKEN_ROW, stride=2), :] = odd[part]
        for row in range(7):
            for iota in range(5):
                tiles[h, row * HALF + iota * 16 : row * HALF + (iota + 1) * 16, :] = spread[
                    pl.ds((h * 7 + row) * HALF + iota, 16, stride=5), :
                ].astype(BF16)

    loads[4].wait()

    def pair_weight(n, carry):
        a, e = n // 3, n % 3
        for part in range(3):
            rows_of = [
                w_mid[pl.ds(pl.multiple_of(((a * 3 + b) * 3 + e) * C + part * 128, 128), 128), :].astype(F32)
                for b in range(3)
            ]
            outer = 0.5 * (rows_of[0] + rows_of[2])
            inner = 0.5 * rows_of[1]
            spot = pl.ds(pl.multiple_of((a * 3 + e) * C + part * 128, 128), 128)
            w_pair[0, spot, :] = (outer + inner).astype(BF16)
            w_pair[1, spot, :] = (outer - inner).astype(BF16)
        return carry

    lax.fori_loop(0, 9, pair_weight, 0)

    top = jnp.where(r == 0, 0.0, 1.0)
    bottom = jnp.where(r == rows - 1, 0.0, 1.0)

    lower = lax.broadcasted_iota(jnp.int32, (5 * HALF, 128), 1) < 64
    def arrive(frames_back):
        for n, (k, d) in enumerate(peers()):
            if k in frames_back:

                @pl.when(source_ok(k, d))
                def _(n=n, k=k, d=d):
                    copy(n, k, d).wait_recv()

        for k in frames_back:
            unfold(k)
            h = BACK - k
            z[h, :, :128] = jnp.where(lower, tiles[h, 2 * HALF :, :], tiles[h, : 5 * HALF, :])
            z[h, :, 128:] = tiles[h, HALF : 6 * HALF, :]

    loads[0].wait()
    loads[3].wait()
    half_gain = 0.5 * gain[...]
    at = lax.broadcasted_iota(jnp.int32, (16, C), 0)

    def shifted_right(values):
        return jnp.where(at == 0, 0.0, pltpu.roll(values, 1, 0)).astype(BF16)

    def shifted_left(values):
        return jnp.where(at == 15, 0.0, pltpu.roll(values, 15, 0)).astype(BF16)

    def put(target, spot, q, iota, value):
        start = (iota + q) * 16
        target[(*spot, slice(start, start + 16), slice(None))] = value.astype(BF16)
        if q == 0 and iota == 0:
            target[(*spot, slice(80, 96), slice(None))] = shifted_left(value)
        if q == 1 and iota == 4:
            target[(*spot, slice(0, 16), slice(None))] = shifted_right(value)

    def convolve(g, result):
        block = jnp.concatenate([z[g], z[g + 1], z[g + 2]], axis=1)
        for p in range(2):
            part = slice(2 * p * C, 2 * (p + 1) * C)
            result[:, part] = jnp.dot(block, w_first[:, part], preferred_element_type=F32)

    def normed(g, result, q, iota, row):
        w, p = row // 2, row % 2
        rounded = result[
            w * HALF + iota * 16 : w * HALF + (iota + 1) * 16, (2 * p + q) * C : (2 * p + q + 1) * C
        ].astype(BF16)
        if g == 2:
            first[q, row, iota * 16 : (iota + 1) * 16, :] = rounded
        value = rounded.astype(F32)
        scale = lax.rsqrt(jnp.mean(value * value, axis=-1, keepdims=True) + 1e-6)
        if row < 2:
            scale = scale * top
        if row >= 8:
            scale = scale * bottom
        value = value * scale * half_gain
        return value + value * jnp.tanh(value)

    def normalize(g, result, pieces=range(10)):
        for piece in pieces:
            q, iota = piece // 5, piece % 5
            target = (n0, n1)[q]
            even = normed(g, result, q, iota, 0)
            odd = normed(g, result, q, iota, 1)
            for pair in range(4):
                next_even = normed(g, result, q, iota, 2 * pair + 2)
                next_odd = normed(g, result, q, iota, 2 * pair + 3)
                put(target, (g, 0, pair), q, iota, even - next_even)
                put(target, (g, 1, pair), q, iota, odd + next_even)
                put(target, (g, 2, pair), q, iota, next_even - odd)
                put(target, (g, 3, pair), q, iota, odd - next_odd)
                even, odd = next_even, next_odd

    arrive((0, 1, 2))
    convolve(2, result_a)
    arrive((3,))
    convolve(1, result_b)
    normalize(2, result_a)
    arrive((4,))
    convolve(0, result_c)
    normalize(1, result_b)

    def taken(views):
        return jnp.concatenate([view.reshape(4 * HALF, C) for view in views], axis=1)

    def accumulate(k, frames_of, fresh):
        def tap(a, e):
            if k == 0 or k == 3:
                start = ((a * 3 + 2 * (k // 3)) * 3 + e) * C
                return w_mid[start : start + C, :]
            start = (a * 3 + e) * C
            return w_pair[k - 1, start : start + C, :]

        weight = jnp.concatenate(
            [
                jnp.concatenate([tap(a, 1 + i), tap(a, i)], axis=1)
                for a in frames_of
                for i in range(2)
            ],
            axis=0,
        )
        views = [v for a in frames_of for v in (n0[a, k, :, :80, :], n1[a, k, :, 16:, :])]
        both = jnp.dot(taken(views), weight, preferred_element_type=F32)
        for q in range(2):
            weight = jnp.concatenate([tap(a, 2 * q) for a in frames_of], axis=0)
            views = [n0[a, k, :, 16:, :] if q == 1 else n1[a, k, :, :80, :] for a in frames_of]
            value = both[:, q * C : (q + 1) * C] + jnp.dot(
                taken(views), weight, preferred_element_type=F32
            )
            if k < 3:
                sums[0, q] = value if fresh and k == 0 else sums[0, q] + value
            if k > 0:
                sums[1, q] = value if fresh and k == 1 else sums[1, q] + (value if k == 1 else -value)

    def mix(parity):
        for q, target in enumerate((m0, m1)):
            for pair in range(4):
                row = 2 * pair + parity
                for iota in range(5):
                    spot = slice(pair * HALF + iota * 16, pair * HALF + (iota + 1) * 16)
                    value = sums[parity, q, spot, :] + first[
                        q, row + 1, iota * 16 : (iota + 1) * 16, :
                    ].astype(F32)
                    if row == 0:
                        value = value * top
                    if row == 7:
                        value = value * bottom
                    put(target, (row,), q, iota, value)
                stores[q][row].start()

    accumulate(0, (1, 2), True)
    normalize(0, result_c)
    accumulate(0, (0,), False)
    for k in range(1, 3):
        accumulate(k, (0, 1, 2), True)
    mix(0)
    accumulate(3, (0, 1, 2), True)
    mix(1)

    for n, (k, d) in enumerate(peers()):

        @pl.when(target_ok(k, d))
        def _(n=n, k=k, d=d):
            copy(n, k, d).wait_send()
    for store in stores[0] + stores[1] + [phase_store]:
        store.wait()


def upsample_kernel(
    m0_hbm, m1_hbm, w_phase_hbm, o_ref, m0, m1, w_phase, d0, d1, turned, out, out_sem, load_sem
):
    loads = [
        pltpu.make_async_copy(m0_hbm, m0, load_sem.at[6]),
        pltpu.make_async_copy(m1_hbm, m1, load_sem.at[7]),
    ]
    phase_loads = [
        pltpu.make_async_copy(w_phase_hbm.at[n], w_phase.at[n], load_sem.at[n]) for n in range(6)
    ]
    for load in loads + phase_loads:
        load.start()
    for load in loads:
        load.wait()
    for difference, source in ((d0, m0), (d1, m1)):
        difference[...] = source[1:] - source[:7]

    def piece(group, n):
        first_iota, count = group
        lanes = pl.ds(pl.multiple_of((n * 30 + first_iota * 6) * 128, 128), count * 6 * 128)
        return pltpu.make_async_copy(out.at[:, :, lanes], o_ref.at[:, :, lanes], out_sem)

    groups = ((0, 3), (3, 2))
    for group in groups:
        first_iota, count = group
        size = count * 16
        plain = slice(first_iota * 16, first_iota * 16 + size)
        after = slice(first_iota * 16 + 16, first_iota * 16 + 16 + size)
        places = (((1, plain), (0, plain), (1, after)), ((0, plain), (1, after), (0, after)))

        def product(pair, row, number, q, v, size=size, places=places):
            taken = jnp.concatenate(
                [
                    pair[parity][row : row + 6, spot, :].reshape(6 * size, C)
                    for parity, spot in places[q][v : v + 2]
                ],
                axis=1,
            )
            if first_iota == 0 and q == 0:
                phase_loads[number].wait()
            return dot_t(taken, w_phase[number])

        for q in range(2):
            centre = [product((m0, m1), 1, v, q, v) for v in range(2)]
            for p in range(2):
                halves = [
                    centre[v] + product((d0, d1), p, 2 + 2 * p + v, q, v) for v in range(2)
                ]
                whole = jnp.concatenate(halves, axis=1)
                for i in range(6):
                    for at in range(count):
                        for t in range(3):
                            start = ((first_iota + at) * 6 + q * 3 + t) * 16 + 2 * i + p
                            turned[pl.ds(start, 16, stride=PITCH), :] = whole[
                                i * size + at * 16 : i * size + (at + 1) * 16, t * 128 : (t + 1) * 128
                            ]

        def write(n, carry, group=group):
            first_iota, count = group
            for t in range(count * 6):
                tile = n * 30 + first_iota * 6 + t
                out[0, :, pl.ds(pl.multiple_of(tile * 128, 128), 128)] = turned[
                    pl.ds(n * PITCH + (first_iota * 6 + t) * 16, 12), :
                ].astype(BF16)
            piece(group, n).start()
            return carry

        lax.fori_loop(0, 16, write, 0)

    pltpu.make_async_copy(out, o_ref, out_sem).wait()


def upsample(m0, m1, w_phase):
    return pl.pallas_call(
        upsample_kernel,
        out_shape=jax.ShapeDtypeStruct((1, 12, 2 * 160 * C_UP), BF16),
        in_specs=[pl.BlockSpec(memory_space=pl.ANY)] * 3,
        out_specs=pl.BlockSpec(memory_space=pl.ANY),
        scratch_shapes=[
            *[pltpu.VMEM((8, 96, C), BF16)] * 2,
            pltpu.VMEM((6, C_UP, 2 * C), BF16),
            *[pltpu.VMEM((7, 96, C), BF16)] * 2,
            pltpu.VMEM((16 * PITCH, 128), F32),
            pltpu.VMEM((1, 12, 2 * 160 * C_UP), BF16),
            pltpu.SemaphoreType.DMA,
            pltpu.SemaphoreType.DMA((8,)),
        ],
        compiler_params=pltpu.CompilerParams(vmem_limit_bytes=UP_LIMIT * 2**20),
        name="upsample",
    )(m0, m1, w_phase)


def on_device(frames, rows, latents, conv_in_weight, gain, conv_mid_weight, up_weight):
    n = len(peers())
    m0, m1, w_phase = pl.pallas_call(
        functools.partial(mix_kernel, frames, rows),
        out_shape=[
            jax.ShapeDtypeStruct((8, 96, C), BF16),
            jax.ShapeDtypeStruct((8, 96, C), BF16),
            jax.ShapeDtypeStruct((6, C_UP, 2 * C), BF16),
        ],
        in_specs=[pl.BlockSpec(memory_space=pl.ANY)] * 5,
        out_specs=[pl.BlockSpec(memory_space=pl.ANY)] * 3,
        scratch_shapes=[
            pltpu.VMEM((3 * TOKEN_ROW, 128), BF16),
            pltpu.VMEM((432, C), BF16),
            pltpu.VMEM((1, C), F32),
            pltpu.VMEM((27 * C, C), BF16),
            pltpu.VMEM((C_UP, 9 * C), BF16),
            pltpu.VMEM((768, 4 * C), BF16),
            pltpu.VMEM((6, C_UP, 2 * C), BF16),
            pltpu.VMEM((2, 9 * C, C), BF16),
            *[pltpu.VMEM((8, 96, C), BF16)] * 2,
            pltpu.VMEM((BACK, 3 * TOKEN_ROW, 128), BF16),
            pltpu.VMEM((BACK + 1, 2 * TOKEN_ROW, 128), BF16),
            pltpu.VMEM((BACK + 1, 2 * TOKEN_ROW, 128), BF16),
            pltpu.VMEM(((BACK + 1) * 7 * HALF, 128), F32),
            pltpu.VMEM((BACK + 1, 7 * HALF, 128), BF16),
            pltpu.VMEM((BACK + 1, 5 * HALF, 256), BF16),
            pltpu.VMEM((2, 10, HALF, C), BF16),
            *[pltpu.VMEM((3, 4, 4, 96, C), BF16)] * 2,
            *[pltpu.VMEM((5 * HALF, 4 * C), F32)] * 3,
            pltpu.VMEM((2, 2, 4 * HALF, C), F32),
            pltpu.SemaphoreType.DMA((n,)),
            pltpu.SemaphoreType.DMA((n,)),
            pltpu.SemaphoreType.DMA((5,)),
            pltpu.SemaphoreType.DMA((17,)),
        ],
        compiler_params=pltpu.CompilerParams(
            collective_id=0, has_side_effects=True, vmem_limit_bytes=MIX_LIMIT * 2**20
        ),
        name="mix",
    )(latents, conv_in_weight, gain, conv_mid_weight, up_weight.T)
    return upsample(m0, m1, w_phase)


def solution(mesh):
    in_specs = (P(("frames", "rows"), None), P(), P(), P(), P())
    out_specs = P("frames", "rows", None)
    return jax.shard_map(
        functools.partial(on_device, mesh.shape["frames"], mesh.shape["rows"]),
        mesh=mesh,
        in_specs=in_specs,
        out_specs=out_specs,
        check_vma=False,
    )
```

```python
import functools

import jax
import jax.numpy as jnp
from jax import lax
from jax.experimental import pallas as pl
from jax.experimental.pallas import tpu as pltpu
from jax.sharding import PartitionSpec as P

F32 = jnp.float32
BF16 = jnp.bfloat16
MESH = pl.DeviceIdType.MESH
C = 384
C_UP = 192
BACK = 4
HALF = 80
PITCH = 481
MIX_LIMIT, UP_LIMIT = 58, 58
TOKEN_ROW = 40


def peers():
    return [(k, d) for k in range(BACK + 1) for d in (-1, 0, 1) if (k, d) != (0, 0)]


def dot_t(left, right):
    return lax.dot_general(left, right, (((1,), (1,)), ((), ())), preferred_element_type=F32)


def mix_kernel(
    frames, rows,
    x_ref, w_in_hbm, gain_hbm, w_mid_hbm, w_up_hbm,
    m0_hbm, m1_hbm, w_phase_hbm,
    mine, w_in, gain, w_mid, w_up, w_first, w_phase, w_pair, m0, m1,
    own, above, below, spread, tiles, z, first, n0, n1, result_a, result_b, result_c, sums,
    send_sem, recv_sem, load_sem, store_sem,
):
    f, r = lax.axis_index("frames"), lax.axis_index("rows")

    def target_ok(k, d):
        return (f + k < frames) & (r + d >= 0) & (r + d < rows)

    def source_ok(k, d):
        return (f - k >= 0) & (r - d >= 0) & (r - d < rows)

    loads = [
        pltpu.make_async_copy(source, target, load_sem.at[n])
        for n, (source, target) in enumerate(
            (
                (x_ref, mine),
                (w_in_hbm, w_in),
                (w_up_hbm, w_up),
                (gain_hbm, gain.at[0]),
                (w_mid_hbm, w_mid),
            )
        )
    ]
    for load in loads:
        load.start()
    barrier = pltpu.get_barrier_semaphore()
    for k, d in peers():

        @pl.when(source_ok(k, d))
        def _(k=k, d=d):
            pl.semaphore_signal(barrier, inc=1, device_id=(f - k, r - d), device_id_type=MESH)

    lane = lax.broadcasted_iota(jnp.int32, (128, 512), 0)
    spot = lax.broadcasted_iota(jnp.int32, (128, 512), 1)
    column = 2 * (lane // 64) + (lane // 16) % 2
    window = (spot // 16) % 4 - column
    part = spot // 128
    wanted = jnp.where(part == 0, 1, jnp.where(part == 1, -1, jnp.where(part == 2, -3, 3)))
    same = ((lane // 32) % 2 == (spot // 64) % 2) & (lane % 16 == spot % 16)
    select = jnp.where(same & (window == wanted), 1.0, 0.0).astype(BF16)

    for k, d in peers():
        dst = own.at[k - 1] if d == 0 else above.at[k] if d == 1 else below.at[k]

        @pl.when(jnp.logical_not(source_ok(k, d)))
        def _(dst=dst):
            dst[...] = jnp.zeros_like(dst)

    loads[1].wait()
    for a in range(3):
        for at, rho in enumerate((3, 0, 1, 2)):
            for kappa in range(4):
                start = a * 256 + at * 64 + kappa * 16
                for p in range(2):
                    for q in range(2):
                        b, e = rho - p, kappa - q
                        spot = (slice(start, start + 16), slice((2 * p + q) * C, (2 * p + q + 1) * C))
                        if 0 <= b <= 2 and 0 <= e <= 2:
                            tap = ((a * 3 + b) * 3 + e) * 16
                            w_first[spot] = w_in[tap : tap + 16, :]
                        else:
                            w_first[spot] = jnp.zeros((16, C), BF16)

    loads[2].wait()
    met = (((0,), (1, 2)), ((0, 1), (2,)))
    for v in range(2):
        for j in range(2):
            spot = slice(j * C, (j + 1) * C)
            by_row = []
            for b in range(3):
                total = None
                for e in met[v][j]:
                    tap = (b * 3 + e) * C
                    term = w_up[:, tap : tap + C].astype(F32)
                    total = term if total is None else total + term
                by_row.append(total)
            w_phase[v, :, spot] = (by_row[0] + by_row[1] + by_row[2]).astype(BF16)
            w_phase[2 + v, :, spot] = (-by_row[0]).astype(BF16)
            w_phase[4 + v, :, spot] = by_row[2].astype(BF16)

    stores = [
        [
            pltpu.make_async_copy(source.at[row], target.at[row], store_sem.at[q * 8 + row])
            for row in range(8)
        ]
        for q, (source, target) in enumerate(((m0, m0_hbm), (m1, m1_hbm)))
    ]
    phase_store = pltpu.make_async_copy(w_phase, w_phase_hbm, store_sem.at[16])
    phase_store.start()

    def as_int(flag):
        return jnp.where(flag, 1, 0)

    sides = 1 + as_int(r > 0) + as_int(r < rows - 1)
    later = 1 + jnp.minimum(frames - 1 - f, BACK)
    pl.semaphore_wait(barrier, sides * later - 1)

    def copy(n, k, d):
        if d == 0:
            src, dst = x_ref, own.at[k - 1]
        elif d == 1:
            src, dst = x_ref.at[TOKEN_ROW:], above.at[k]
        else:
            src, dst = x_ref.at[: 2 * TOKEN_ROW], below.at[k]
        return pltpu.make_async_remote_copy(
            src_ref=src,
            dst_ref=dst,
            send_sem=send_sem.at[n],
            recv_sem=recv_sem.at[n],
            device_id=(f + k, r + d),
            device_id_type=MESH,
        )

    for n, (k, d) in enumerate(peers()):

        @pl.when(target_ok(k, d))
        def _(n=n, k=k, d=d):
            copy(n, k, d).start()

    token = lax.broadcasted_iota(jnp.int32, (7 * TOKEN_ROW, 128), 0) % TOKEN_ROW

    def unfold(k):
        h = BACK - k
        own_band = mine[...] if k == 0 else own[k - 1]
        block = jnp.concatenate([above[k], below[k], own_band], axis=0)
        got = jnp.dot(block, select, preferred_element_type=F32)
        left = jnp.where(token == 0, 0.0, pltpu.roll(got[:, 256:384], 1, 0))
        right = jnp.where(token == TOKEN_ROW - 1, 0.0, pltpu.roll(got[:, 384:], 7 * TOKEN_ROW - 1, 0))
        even, odd = got[:, :128] + left, got[:, 128:256] + right
        for n, row in enumerate((0, 1, 5, 6, 2, 3, 4)):
            part = slice(n * TOKEN_ROW, (n + 1) * TOKEN_ROW)
            start = (h * 7 + row) * HALF
            spread[pl.ds(start, TOKEN_ROW, stride=2), :] = even[part]
            spread[pl.ds(start + 1, TOKEN_ROW, stride=2), :] = odd[part]
        for row in range(7):
            for iota in range(5):
                tiles[h, row * HALF + iota * 16 : row * HALF + (iota + 1) * 16, :] = spread[
                    pl.ds((h * 7 + row) * HALF + iota, 16, stride=5), :
                ].astype(BF16)

    loads[4].wait()

    def pair_weight(n, carry):
        a, e = n // 3, n % 3
        for part in range(3):
            rows_of = [
                w_mid[pl.ds(pl.multiple_of(((a * 3 + b) * 3 + e) * C + part * 128, 128), 128), :].astype(F32)
                for b in range(3)
            ]
            outer = 0.5 * (rows_of[0] + rows_of[2])
            inner = 0.5 * rows_of[1]
            spot = pl.ds(pl.multiple_of((a * 3 + e) * C + part * 128, 128), 128)
            w_pair[0, spot, :] = (outer + inner).astype(BF16)
            w_pair[1, spot, :] = (outer - inner).astype(BF16)
        return carry

    lax.fori_loop(0, 9, pair_weight, 0)

    top = jnp.where(r == 0, 0.0, 1.0)
    bottom = jnp.where(r == rows - 1, 0.0, 1.0)

    lower = lax.broadcasted_iota(jnp.int32, (5 * HALF, 128), 1) < 64
    def arrive(frames_back):
        for n, (k, d) in enumerate(peers()):
            if k in frames_back:

                @pl.when(source_ok(k, d))
                def _(n=n, k=k, d=d):
                    copy(n, k, d).wait_recv()

        for k in frames_back:
            unfold(k)
            h = BACK - k
            z[h, :, :128] = jnp.where(lower, tiles[h, 2 * HALF :, :], tiles[h, : 5 * HALF, :])
            z[h, :, 128:] = tiles[h, HALF : 6 * HALF, :]

    loads[0].wait()
    loads[3].wait()
    half_gain = 0.5 * gain[...]
    at = lax.broadcasted_iota(jnp.int32, (16, C), 0)

    def shifted_right(values):
        return jnp.where(at == 0, 0.0, pltpu.roll(values, 1, 0)).astype(BF16)

    def shifted_left(values):
        return jnp.where(at == 15, 0.0, pltpu.roll(values, 15, 0)).astype(BF16)

    def put(target, spot, q, iota, value):
        start = (iota + q) * 16
        target[(*spot, slice(start, start + 16), slice(None))] = value.astype(BF16)
        if q == 0 and iota == 0:
            target[(*spot, slice(80, 96), slice(None))] = shifted_left(value)
        if q == 1 and iota == 4:
            target[(*spot, slice(0, 16), slice(None))] = shifted_right(value)

    def convolve(g, result):
        block = jnp.concatenate([z[g], z[g + 1], z[g + 2]], axis=1)
        for p in range(2):
            part = slice(2 * p * C, 2 * (p + 1) * C)
            result[:, part] = jnp.dot(block, w_first[:, part], preferred_element_type=F32)

    def normed(g, result, q, iota, row):
        w, p = row // 2, row % 2
        rounded = result[
            w * HALF + iota * 16 : w * HALF + (iota + 1) * 16, (2 * p + q) * C : (2 * p + q + 1) * C
        ].astype(BF16)
        if g == 2:
            first[q, row, iota * 16 : (iota + 1) * 16, :] = rounded
        value = rounded.astype(F32)
        scale = lax.rsqrt(jnp.mean(value * value, axis=-1, keepdims=True) + 1e-6)
        if row < 2:
            scale = scale * top
        if row >= 8:
            scale = scale * bottom
        value = value * scale * half_gain
        return value + value * jnp.tanh(value)

    def normalize(g, result, pieces=range(10)):
        for piece in pieces:
            q, iota = piece // 5, piece % 5
            target = (n0, n1)[q]
            even = normed(g, result, q, iota, 0)
            odd = normed(g, result, q, iota, 1)
            for pair in range(4):
                next_even = normed(g, result, q, iota, 2 * pair + 2)
                next_odd = normed(g, result, q, iota, 2 * pair + 3)
                put(target, (g, 0, pair), q, iota, even - next_even)
                put(target, (g, 1, pair), q, iota, odd + next_even)
                put(target, (g, 2, pair), q, iota, next_even - odd)
                put(target, (g, 3, pair), q, iota, odd - next_odd)
                even, odd = next_even, next_odd

    arrive((0, 1))
    arrive((2,))
    convolve(2, result_a)
    arrive((3,))
    convolve(1, result_b)
    normalize(2, result_a)
    arrive((4,))
    convolve(0, result_c)
    normalize(1, result_b)

    def taken(views):
        return jnp.concatenate([view.reshape(4 * HALF, C) for view in views], axis=1)

    def accumulate(k, frames_of, fresh):
        def tap(a, e):
            if k == 0 or k == 3:
                start = ((a * 3 + 2 * (k // 3)) * 3 + e) * C
                return w_mid[start : start + C, :]
            start = (a * 3 + e) * C
            return w_pair[k - 1, start : start + C, :]

        weight = jnp.concatenate(
            [
                jnp.concatenate([tap(a, 1 + i), tap(a, i)], axis=1)
                for a in frames_of
                for i in range(2)
            ],
            axis=0,
        )
        views = [v for a in frames_of for v in (n0[a, k, :, :80, :], n1[a, k, :, 16:, :])]
        both = jnp.dot(taken(views), weight, preferred_element_type=F32)
        for q in range(2):
            weight = jnp.concatenate([tap(a, 2 * q) for a in frames_of], axis=0)
            views = [n0[a, k, :, 16:, :] if q == 1 else n1[a, k, :, :80, :] for a in frames_of]
            value = both[:, q * C : (q + 1) * C] + jnp.dot(
                taken(views), weight, preferred_element_type=F32
            )
            if k < 3:
                sums[0, q] = value if fresh and k == 0 else sums[0, q] + value
            if k > 0:
                sums[1, q] = value if fresh and k == 1 else sums[1, q] + (value if k == 1 else -value)

    def mix(parity):
        for q, target in enumerate((m0, m1)):
            for pair in range(4):
                row = 2 * pair + parity
                for iota in range(5):
                    spot = slice(pair * HALF + iota * 16, pair * HALF + (iota + 1) * 16)
                    value = sums[parity, q, spot, :] + first[
                        q, row + 1, iota * 16 : (iota + 1) * 16, :
                    ].astype(F32)
                    if row == 0:
                        value = value * top
                    if row == 7:
                        value = value * bottom
                    put(target, (row,), q, iota, value)
                stores[q][row].start()

    accumulate(0, (1, 2), True)
    normalize(0, result_c)
    accumulate(0, (0,), False)
    for k in range(1, 3):
        accumulate(k, (0, 1, 2), True)
    mix(0)
    accumulate(3, (0, 1, 2), True)
    mix(1)

    for n, (k, d) in enumerate(peers()):

        @pl.when(target_ok(k, d))
        def _(n=n, k=k, d=d):
            copy(n, k, d).wait_send()
    for store in stores[0] + stores[1] + [phase_store]:
        store.wait()


def upsample_kernel(
    m0_hbm, m1_hbm, w_phase_hbm, o_ref, m0, m1, w_phase, d0, d1, turned, out, out_sem, load_sem
):
    loads = [
        pltpu.make_async_copy(m0_hbm, m0, load_sem.at[6]),
        pltpu.make_async_copy(m1_hbm, m1, load_sem.at[7]),
    ]
    phase_loads = [
        pltpu.make_async_copy(w_phase_hbm.at[n], w_phase.at[n], load_sem.at[n]) for n in range(6)
    ]
    for load in loads + phase_loads:
        load.start()
    for load in loads:
        load.wait()
    for difference, source in ((d0, m0), (d1, m1)):
        difference[...] = source[1:] - source[:7]

    def piece(group, n):
        first_iota, count = group
        lanes = pl.ds(pl.multiple_of((n * 30 + first_iota * 6) * 128, 128), count * 6 * 128)
        return pltpu.make_async_copy(out.at[:, :, lanes], o_ref.at[:, :, lanes], out_sem)

    groups = ((0, 3), (3, 2))
    for group in groups:
        first_iota, count = group
        size = count * 16
        plain = slice(first_iota * 16, first_iota * 16 + size)
        after = slice(first_iota * 16 + 16, first_iota * 16 + 16 + size)
        places = (((1, plain), (0, plain), (1, after)), ((0, plain), (1, after), (0, after)))

        def product(pair, row, number, q, v, size=size, places=places):
            taken = jnp.concatenate(
                [
                    pair[parity][row : row + 6, spot, :].reshape(6 * size, C)
                    for parity, spot in places[q][v : v + 2]
                ],
                axis=1,
            )
            if first_iota == 0 and q == 0:
                phase_loads[number].wait()
            return dot_t(taken, w_phase[number])

        for q in range(2):
            centre = [product((m0, m1), 1, v, q, v) for v in range(2)]
            for p in range(2):
                halves = [
                    centre[v] + product((d0, d1), p, 2 + 2 * p + v, q, v) for v in range(2)
                ]
                whole = jnp.concatenate(halves, axis=1)
                for i in range(6):
                    for at in range(count):
                        for t in range(3):
                            start = ((first_iota + at) * 6 + q * 3 + t) * 16 + 2 * i + p
                            turned[pl.ds(start, 16, stride=PITCH), :] = whole[
                                i * size + at * 16 : i * size + (at + 1) * 16, t * 128 : (t + 1) * 128
                            ]

        def write(n, carry, group=group):
            first_iota, count = group
            for t in range(count * 6):
                tile = n * 30 + first_iota * 6 + t
                out[0, :, pl.ds(pl.multiple_of(tile * 128, 128), 128)] = turned[
                    pl.ds(n * PITCH + (first_iota * 6 + t) * 16, 12), :
                ].astype(BF16)
            piece(group, n).start()
            return carry

        lax.fori_loop(0, 16, write, 0)

    pltpu.make_async_copy(out, o_ref, out_sem).wait()


def upsample(m0, m1, w_phase):
    return pl.pallas_call(
        upsample_kernel,
        out_shape=jax.ShapeDtypeStruct((1, 12, 2 * 160 * C_UP), BF16),
        in_specs=[pl.BlockSpec(memory_space=pl.ANY)] * 3,
        out_specs=pl.BlockSpec(memory_space=pl.ANY),
        scratch_shapes=[
            *[pltpu.VMEM((8, 96, C), BF16)] * 2,
            pltpu.VMEM((6, C_UP, 2 * C), BF16),
            *[pltpu.VMEM((7, 96, C), BF16)] * 2,
            pltpu.VMEM((17 * PITCH, 128), F32),
            pltpu.VMEM((1, 12, 2 * 160 * C_UP), BF16),
            pltpu.SemaphoreType.DMA,
            pltpu.SemaphoreType.DMA((8,)),
        ],
        compiler_params=pltpu.CompilerParams(vmem_limit_bytes=UP_LIMIT * 2**20),
        name="upsample",
    )(m0, m1, w_phase)


def on_device(frames, rows, latents, conv_in_weight, gain, conv_mid_weight, up_weight):
    n = len(peers())
    m0, m1, w_phase = pl.pallas_call(
        functools.partial(mix_kernel, frames, rows),
        out_shape=[
            jax.ShapeDtypeStruct((8, 96, C), BF16),
            jax.ShapeDtypeStruct((8, 96, C), BF16),
            jax.ShapeDtypeStruct((6, C_UP, 2 * C), BF16),
        ],
        in_specs=[pl.BlockSpec(memory_space=pl.ANY)] * 5,
        out_specs=[pl.BlockSpec(memory_space=pl.ANY)] * 3,
        scratch_shapes=[
            pltpu.VMEM((3 * TOKEN_ROW, 128), BF16),
            pltpu.VMEM((432, C), BF16),
            pltpu.VMEM((1, C), F32),
            pltpu.VMEM((27 * C, C), BF16),
            pltpu.VMEM((C_UP, 9 * C), BF16),
            pltpu.VMEM((768, 4 * C), BF16),
            pltpu.VMEM((6, C_UP, 2 * C), BF16),
            pltpu.VMEM((2, 9 * C, C), BF16),
            *[pltpu.VMEM((8, 96, C), BF16)] * 2,
            pltpu.VMEM((BACK, 3 * TOKEN_ROW, 128), BF16),
            pltpu.VMEM((BACK + 1, 2 * TOKEN_ROW, 128), BF16),
            pltpu.VMEM((BACK + 1, 2 * TOKEN_ROW, 128), BF16),
            pltpu.VMEM(((BACK + 1) * 7 * HALF + 16, 128), F32),
            pltpu.VMEM((BACK + 1, 7 * HALF, 128), BF16),
            pltpu.VMEM((BACK + 1, 5 * HALF, 256), BF16),
            pltpu.VMEM((2, 10, HALF, C), BF16),
            *[pltpu.VMEM((3, 4, 4, 96, C), BF16)] * 2,
            *[pltpu.VMEM((5 * HALF, 4 * C), F32)] * 3,
            pltpu.VMEM((2, 2, 4 * HALF, C), F32),
            pltpu.SemaphoreType.DMA((n,)),
            pltpu.SemaphoreType.DMA((n,)),
            pltpu.SemaphoreType.DMA((5,)),
            pltpu.SemaphoreType.DMA((17,)),
        ],
        compiler_params=pltpu.CompilerParams(
            collective_id=0, has_side_effects=True, vmem_limit_bytes=MIX_LIMIT * 2**20
        ),
        name="mix",
    )(latents, conv_in_weight, gain, conv_mid_weight, up_weight.T)
    return upsample(m0, m1, w_phase)


def solution(mesh):
    in_specs = (P(("frames", "rows"), None), P(), P(), P(), P())
    out_specs = P("frames", "rows", None)
    return jax.shard_map(
        functools.partial(on_device, mesh.shape["frames"], mesh.shape["rows"]),
        mesh=mesh,
        in_specs=in_specs,
        out_specs=out_specs,
        check_vma=False,
    )
```

```python
import functools

import jax
import jax.numpy as jnp
from jax import lax
from jax.experimental import pallas as pl
from jax.experimental.pallas import tpu as pltpu
from jax.sharding import PartitionSpec as P

F32 = jnp.float32
BF16 = jnp.bfloat16
MESH = pl.DeviceIdType.MESH
C = 384
C_UP = 192
BACK = 4
HALF = 80
PITCH = 481
MIX_LIMIT, UP_LIMIT = 58, 58
TOKEN_ROW = 40


def peers():
    return [(k, d) for k in range(BACK + 1) for d in (-1, 0, 1) if (k, d) != (0, 0)]


def dot_t(left, right):
    return lax.dot_general(left, right, (((1,), (1,)), ((), ())), preferred_element_type=F32)


def mix_kernel(
    frames, rows,
    x_ref, w_in_hbm, gain_hbm, w_mid_hbm, w_up_hbm,
    m0_hbm, m1_hbm, w_phase_hbm,
    mine, w_in, gain, w_mid, w_up, w_first, w_phase, w_pair, m0, m1,
    own, above, below, spread, tiles, z, first, n0, n1, result_a, result_b, result_c, sums,
    send_sem, recv_sem, load_sem, store_sem,
):
    f, r = lax.axis_index("frames"), lax.axis_index("rows")

    def target_ok(k, d):
        return (f + k < frames) & (r + d >= 0) & (r + d < rows)

    def source_ok(k, d):
        return (f - k >= 0) & (r - d >= 0) & (r - d < rows)

    loads = [
        pltpu.make_async_copy(source, target, load_sem.at[n])
        for n, (source, target) in enumerate(
            (
                (x_ref, mine),
                (w_in_hbm, w_in),
                (w_up_hbm, w_up),
                (gain_hbm, gain.at[0]),
                (w_mid_hbm, w_mid),
            )
        )
    ]
    for load in loads:
        load.start()
    barrier = pltpu.get_barrier_semaphore()
    for k, d in peers():

        @pl.when(source_ok(k, d))
        def _(k=k, d=d):
            pl.semaphore_signal(barrier, inc=1, device_id=(f - k, r - d), device_id_type=MESH)

    lane = lax.broadcasted_iota(jnp.int32, (128, 512), 0)
    spot = lax.broadcasted_iota(jnp.int32, (128, 512), 1)
    column = 2 * (lane // 64) + (lane // 16) % 2
    window = (spot // 16) % 4 - column
    part = spot // 128
    wanted = jnp.where(part == 0, 1, jnp.where(part == 1, -1, jnp.where(part == 2, -3, 3)))
    same = ((lane // 32) % 2 == (spot // 64) % 2) & (lane % 16 == spot % 16)
    select = jnp.where(same & (window == wanted), 1.0, 0.0).astype(BF16)

    for k, d in peers():
        dst = own.at[k - 1] if d == 0 else above.at[k] if d == 1 else below.at[k]

        @pl.when(jnp.logical_not(source_ok(k, d)))
        def _(dst=dst):
            dst[...] = jnp.zeros_like(dst)

    loads[1].wait()
    for a in range(3):
        for at, rho in enumerate((3, 0, 1, 2)):
            for kappa in range(4):
                start = a * 256 + at * 64 + kappa * 16
                for p in range(2):
                    for q in range(2):
                        b, e = rho - p, kappa - q
                        spot = (slice(start, start + 16), slice((2 * p + q) * C, (2 * p + q + 1) * C))
                        if 0 <= b <= 2 and 0 <= e <= 2:
                            tap = ((a * 3 + b) * 3 + e) * 16
                            w_first[spot] = w_in[tap : tap + 16, :]
                        else:
                            w_first[spot] = jnp.zeros((16, C), BF16)

    loads[2].wait()
    met = (((0,), (1, 2)), ((0, 1), (2,)))
    for v in range(2):
        for j in range(2):
            spot = slice(j * C, (j + 1) * C)
            by_row = []
            for b in range(3):
                total = None
                for e in met[v][j]:
                    tap = (b * 3 + e) * C
                    term = w_up[:, tap : tap + C].astype(F32)
                    total = term if total is None else total + term
                by_row.append(total)
            w_phase[v, :, spot] = (by_row[0] + by_row[1] + by_row[2]).astype(BF16)
            w_phase[2 + v, :, spot] = (-by_row[0]).astype(BF16)
            w_phase[4 + v, :, spot] = by_row[2].astype(BF16)

    stores = [
        [
            pltpu.make_async_copy(source.at[row], target.at[row], store_sem.at[q * 8 + row])
            for row in range(8)
        ]
        for q, (source, target) in enumerate(((m0, m0_hbm), (m1, m1_hbm)))
    ]
    phase_store = pltpu.make_async_copy(w_phase, w_phase_hbm, store_sem.at[16])
    phase_store.start()

    def as_int(flag):
        return jnp.where(flag, 1, 0)

    sides = 1 + as_int(r > 0) + as_int(r < rows - 1)
    later = 1 + jnp.minimum(frames - 1 - f, BACK)
    pl.semaphore_wait(barrier, sides * later - 1)

    def copy(n, k, d):
        if d == 0:
            src, dst = x_ref, own.at[k - 1]
        elif d == 1:
            src, dst = x_ref.at[TOKEN_ROW:], above.at[k]
        else:
            src, dst = x_ref.at[: 2 * TOKEN_ROW], below.at[k]
        return pltpu.make_async_remote_copy(
            src_ref=src,
            dst_ref=dst,
            send_sem=send_sem.at[n],
            recv_sem=recv_sem.at[n],
            device_id=(f + k, r + d),
            device_id_type=MESH,
        )

    for n, (k, d) in enumerate(peers()):

        @pl.when(target_ok(k, d))
        def _(n=n, k=k, d=d):
            copy(n, k, d).start()

    token = lax.broadcasted_iota(jnp.int32, (7 * TOKEN_ROW, 128), 0) % TOKEN_ROW

    def unfold(k):
        h = BACK - k
        own_band = mine[...] if k == 0 else own[k - 1]
        block = jnp.concatenate([above[k], below[k], own_band], axis=0)
        got = jnp.dot(block, select, preferred_element_type=F32)
        left = jnp.where(token == 0, 0.0, pltpu.roll(got[:, 256:384], 1, 0))
        right = jnp.where(token == TOKEN_ROW - 1, 0.0, pltpu.roll(got[:, 384:], 7 * TOKEN_ROW - 1, 0))
        even, odd = got[:, :128] + left, got[:, 128:256] + right
        for n, row in enumerate((0, 1, 5, 6, 2, 3, 4)):
            part = slice(n * TOKEN_ROW, (n + 1) * TOKEN_ROW)
            start = (h * 7 + row) * HALF
            spread[pl.ds(start, TOKEN_ROW, stride=2), :] = even[part]
            spread[pl.ds(start + 1, TOKEN_ROW, stride=2), :] = odd[part]
        for row in range(7):
            for iota in range(5):
                tiles[h, row * HALF + iota * 16 : row * HALF + (iota + 1) * 16, :] = spread[
                    pl.ds((h * 7 + row) * HALF + iota, 16, stride=5), :
                ].astype(BF16)

    loads[4].wait()

    def pair_weight(n, carry):
        a, e = n // 3, n % 3
        for part in range(3):
            rows_of = [
                w_mid[pl.ds(pl.multiple_of(((a * 3 + b) * 3 + e) * C + part * 128, 128), 128), :].astype(F32)
                for b in range(3)
            ]
            outer = 0.5 * (rows_of[0] + rows_of[2])
            inner = 0.5 * rows_of[1]
            spot = pl.ds(pl.multiple_of((a * 3 + e) * C + part * 128, 128), 128)
            w_pair[0, spot, :] = (outer + inner).astype(BF16)
            w_pair[1, spot, :] = (outer - inner).astype(BF16)
        return carry

    lax.fori_loop(0, 9, pair_weight, 0)

    top = jnp.where(r == 0, 0.0, 1.0)
    bottom = jnp.where(r == rows - 1, 0.0, 1.0)

    lower = lax.broadcasted_iota(jnp.int32, (5 * HALF, 128), 1) < 64
    def arrive(frames_back):
        for n, (k, d) in enumerate(peers()):
            if k in frames_back:

                @pl.when(source_ok(k, d))
                def _(n=n, k=k, d=d):
                    copy(n, k, d).wait_recv()

        for k in frames_back:
            unfold(k)
            h = BACK - k
            z[h, :, :128] = jnp.where(lower, tiles[h, 2 * HALF :, :], tiles[h, : 5 * HALF, :])
            z[h, :, 128:] = tiles[h, HALF : 6 * HALF, :]

    loads[0].wait()
    loads[3].wait()
    half_gain = 0.5 * gain[...]
    at = lax.broadcasted_iota(jnp.int32, (16, C), 0)

    def shifted_right(values):
        return jnp.where(at == 0, 0.0, pltpu.roll(values.astype(F32), 1, 0)).astype(BF16)

    def shifted_left(values):
        return jnp.where(at == 15, 0.0, pltpu.roll(values.astype(F32), 15, 0)).astype(BF16)

    def put(target, spot, q, iota, value):
        start = (iota + q) * 16
        target[(*spot, slice(start, start + 16), slice(None))] = value.astype(BF16)
        if q == 0 and iota == 0:
            target[(*spot, slice(80, 96), slice(None))] = shifted_left(value)
        if q == 1 and iota == 4:
            target[(*spot, slice(0, 16), slice(None))] = shifted_right(value)

    def convolve(g, result):
        block = jnp.concatenate([z[g], z[g + 1], z[g + 2]], axis=1)
        for p in range(2):
            part = slice(2 * p * C, 2 * (p + 1) * C)
            result[:, part] = jnp.dot(block, w_first[:, part], preferred_element_type=F32)

    def normed(g, result, q, iota, row):
        w, p = row // 2, row % 2
        rounded = result[
            w * HALF + iota * 16 : w * HALF + (iota + 1) * 16, (2 * p + q) * C : (2 * p + q + 1) * C
        ].astype(BF16)
        if g == 2:
            first[q, row, iota * 16 : (iota + 1) * 16, :] = rounded
        value = rounded.astype(F32)
        scale = lax.rsqrt(jnp.mean(value * value, axis=-1, keepdims=True) + 1e-6)
        if row < 2:
            scale = scale * top
        if row >= 8:
            scale = scale * bottom
        value = value * scale * half_gain
        return (value + value * jnp.tanh(value)).astype(BF16)

    def normalize(g, result, pieces=range(10)):
        for piece in pieces:
            q, iota = piece // 5, piece % 5
            target = (n0, n1)[q]
            even = normed(g, result, q, iota, 0)
            odd = normed(g, result, q, iota, 1)
            for pair in range(4):
                next_even = normed(g, result, q, iota, 2 * pair + 2)
                next_odd = normed(g, result, q, iota, 2 * pair + 3)
                put(target, (g, 0, pair), q, iota, even - next_even)
                put(target, (g, 1, pair), q, iota, odd + next_even)
                put(target, (g, 2, pair), q, iota, next_even - odd)
                put(target, (g, 3, pair), q, iota, odd - next_odd)
                even, odd = next_even, next_odd

    arrive((0, 1))
    arrive((2,))
    convolve(2, result_a)
    arrive((3,))
    convolve(1, result_b)
    normalize(2, result_a)
    arrive((4,))
    convolve(0, result_c)
    normalize(1, result_b)

    def taken(views):
        return jnp.concatenate([view.reshape(4 * HALF, C) for view in views], axis=1)

    def accumulate(k, frames_of, fresh):
        def tap(a, e):
            if k == 0 or k == 3:
                start = ((a * 3 + 2 * (k // 3)) * 3 + e) * C
                return w_mid[start : start + C, :]
            start = (a * 3 + e) * C
            return w_pair[k - 1, start : start + C, :]

        weight = jnp.concatenate(
            [
                jnp.concatenate([tap(a, 1 + i), tap(a, i)], axis=1)
                for a in frames_of
                for i in range(2)
            ],
            axis=0,
        )
        views = [v for a in frames_of for v in (n0[a, k, :, :80, :], n1[a, k, :, 16:, :])]
        both = jnp.dot(taken(views), weight, preferred_element_type=F32)
        for q in range(2):
            weight = jnp.concatenate([tap(a, 2 * q) for a in frames_of], axis=0)
            views = [n0[a, k, :, 16:, :] if q == 1 else n1[a, k, :, :80, :] for a in frames_of]
            value = both[:, q * C : (q + 1) * C] + jnp.dot(
                taken(views), weight, preferred_element_type=F32
            )
            if k < 3:
                sums[0, q] = value if fresh and k == 0 else sums[0, q] + value
            if k > 0:
                sums[1, q] = value if fresh and k == 1 else sums[1, q] + (value if k == 1 else -value)

    def mix(parity):
        for q, target in enumerate((m0, m1)):
            for pair in range(4):
                row = 2 * pair + parity
                for iota in range(5):
                    spot = slice(pair * HALF + iota * 16, pair * HALF + (iota + 1) * 16)
                    value = sums[parity, q, spot, :] + first[
                        q, row + 1, iota * 16 : (iota + 1) * 16, :
                    ].astype(F32)
                    if row == 0:
                        value = value * top
                    if row == 7:
                        value = value * bottom
                    put(target, (row,), q, iota, value)
                stores[q][row].start()

    accumulate(0, (1, 2), True)
    normalize(0, result_c)
    accumulate(0, (0,), False)
    for k in range(1, 3):
        accumulate(k, (0, 1, 2), True)
    mix(0)
    accumulate(3, (0, 1, 2), True)
    mix(1)

    for n, (k, d) in enumerate(peers()):

        @pl.when(target_ok(k, d))
        def _(n=n, k=k, d=d):
            copy(n, k, d).wait_send()
    for store in stores[0] + stores[1] + [phase_store]:
        store.wait()


def upsample_kernel(
    m0_hbm, m1_hbm, w_phase_hbm, o_ref, m0, m1, w_phase, d0, d1, turned, out, out_sem, load_sem
):
    loads = [
        pltpu.make_async_copy(m0_hbm, m0, load_sem.at[6]),
        pltpu.make_async_copy(m1_hbm, m1, load_sem.at[7]),
    ]
    phase_loads = [
        pltpu.make_async_copy(w_phase_hbm.at[n], w_phase.at[n], load_sem.at[n]) for n in range(6)
    ]
    for load in loads + phase_loads:
        load.start()
    for load in loads:
        load.wait()
    for difference, source in ((d0, m0), (d1, m1)):
        difference[...] = source[1:] - source[:7]

    def piece(group, n):
        first_iota, count = group
        lanes = pl.ds(pl.multiple_of((n * 30 + first_iota * 6) * 128, 128), count * 6 * 128)
        return pltpu.make_async_copy(out.at[:, :, lanes], o_ref.at[:, :, lanes], out_sem)

    groups = ((0, 3), (3, 2))
    for group in groups:
        first_iota, count = group
        size = count * 16
        plain = slice(first_iota * 16, first_iota * 16 + size)
        after = slice(first_iota * 16 + 16, first_iota * 16 + 16 + size)
        places = (((1, plain), (0, plain), (1, after)), ((0, plain), (1, after), (0, after)))

        def product(pair, row, number, q, v, size=size, places=places):
            taken = jnp.concatenate(
                [
                    pair[parity][row : row + 6, spot, :].reshape(6 * size, C)
                    for parity, spot in places[q][v : v + 2]
                ],
                axis=1,
            )
            if first_iota == 0 and q == 0:
                phase_loads[number].wait()
            return dot_t(taken, w_phase[number])

        for q in range(2):
            centre = [product((m0, m1), 1, v, q, v) for v in range(2)]
            for p in range(2):
                halves = [
                    centre[v] + product((d0, d1), p, 2 + 2 * p + v, q, v) for v in range(2)
                ]
                whole = jnp.concatenate(halves, axis=1)
                for i in range(6):
                    for at in range(count):
                        for t in range(3):
                            start = ((first_iota + at) * 6 + q * 3 + t) * 16 + 2 * i + p
                            turned[pl.ds(start, 16, stride=PITCH), :] = whole[
                                i * size + at * 16 : i * size + (at + 1) * 16, t * 128 : (t + 1) * 128
                            ]

        def write(n, carry, group=group):
            first_iota, count = group
            for t in range(count * 6):
                tile = n * 30 + first_iota * 6 + t
                out[0, :, pl.ds(pl.multiple_of(tile * 128, 128), 128)] = turned[
                    pl.ds(n * PITCH + (first_iota * 6 + t) * 16, 12), :
                ].astype(BF16)
            piece(group, n).start()
            return carry

        lax.fori_loop(0, 16, write, 0)

    pltpu.make_async_copy(out, o_ref, out_sem).wait()


def upsample(m0, m1, w_phase):
    return pl.pallas_call(
        upsample_kernel,
        out_shape=jax.ShapeDtypeStruct((1, 12, 2 * 160 * C_UP), BF16),
        in_specs=[pl.BlockSpec(memory_space=pl.ANY)] * 3,
        out_specs=pl.BlockSpec(memory_space=pl.ANY),
        scratch_shapes=[
            *[pltpu.VMEM((8, 96, C), BF16)] * 2,
            pltpu.VMEM((6, C_UP, 2 * C), BF16),
            *[pltpu.VMEM((7, 96, C), BF16)] * 2,
            pltpu.VMEM((17 * PITCH, 128), F32),
            pltpu.VMEM((1, 12, 2 * 160 * C_UP), BF16),
            pltpu.SemaphoreType.DMA,
            pltpu.SemaphoreType.DMA((8,)),
        ],
        compiler_params=pltpu.CompilerParams(vmem_limit_bytes=UP_LIMIT * 2**20),
        name="upsample",
    )(m0, m1, w_phase)


def on_device(frames, rows, latents, conv_in_weight, gain, conv_mid_weight, up_weight):
    n = len(peers())
    m0, m1, w_phase = pl.pallas_call(
        functools.partial(mix_kernel, frames, rows),
        out_shape=[
            jax.ShapeDtypeStruct((8, 96, C), BF16),
            jax.ShapeDtypeStruct((8, 96, C), BF16),
            jax.ShapeDtypeStruct((6, C_UP, 2 * C), BF16),
        ],
        in_specs=[pl.BlockSpec(memory_space=pl.ANY)] * 5,
        out_specs=[pl.BlockSpec(memory_space=pl.ANY)] * 3,
        scratch_shapes=[
            pltpu.VMEM((3 * TOKEN_ROW, 128), BF16),
            pltpu.VMEM((432, C), BF16),
            pltpu.VMEM((1, C), F32),
            pltpu.VMEM((27 * C, C), BF16),
            pltpu.VMEM((C_UP, 9 * C), BF16),
            pltpu.VMEM((768, 4 * C), BF16),
            pltpu.VMEM((6, C_UP, 2 * C), BF16),
            pltpu.VMEM((2, 9 * C, C), BF16),
            *[pltpu.VMEM((8, 96, C), BF16)] * 2,
            pltpu.VMEM((BACK, 3 * TOKEN_ROW, 128), BF16),
            pltpu.VMEM((BACK + 1, 2 * TOKEN_ROW, 128), BF16),
            pltpu.VMEM((BACK + 1, 2 * TOKEN_ROW, 128), BF16),
            pltpu.VMEM(((BACK + 1) * 7 * HALF + 16, 128), F32),
            pltpu.VMEM((BACK + 1, 7 * HALF, 128), BF16),
            pltpu.VMEM((BACK + 1, 5 * HALF, 256), BF16),
            pltpu.VMEM((2, 10, HALF, C), BF16),
            *[pltpu.VMEM((3, 4, 4, 96, C), BF16)] * 2,
            *[pltpu.VMEM((5 * HALF, 4 * C), F32)] * 3,
            pltpu.VMEM((2, 2, 4 * HALF, C), F32),
            pltpu.SemaphoreType.DMA((n,)),
            pltpu.SemaphoreType.DMA((n,)),
            pltpu.SemaphoreType.DMA((5,)),
            pltpu.SemaphoreType.DMA((17,)),
        ],
        compiler_params=pltpu.CompilerParams(
            collective_id=0, has_side_effects=True, vmem_limit_bytes=MIX_LIMIT * 2**20
        ),
        name="mix",
    )(latents, conv_in_weight, gain, conv_mid_weight, up_weight.T)
    return upsample(m0, m1, w_phase)


def solution(mesh):
    in_specs = (P(("frames", "rows"), None), P(), P(), P(), P())
    out_specs = P("frames", "rows", None)
    return jax.shard_map(
        functools.partial(on_device, mesh.shape["frames"], mesh.shape["rows"]),
        mesh=mesh,
        in_specs=in_specs,
        out_specs=out_specs,
        check_vma=False,
    )
```
